1024 devices in a mesh: ia: 4 (over x_lo, core), ja: 8 (over y), ka: 32 (over z, x_hi).
Axes of the slice: x: 8 (x_hi: 4, x_lo: 2; x = x_hi * 2 + x_lo), y: 8, z: 8, core: 2. Of those that a mesh axis runs over, the one named last changes fastest.
Arguments:
- tensor: float32 [16, 2048, 8192], P('ia', 'ja', 'ka'), may hold values from -6 to 6
- factor_a: float32 [16, 64], replicated, may hold values from -0.03125 to 0.03125
- factor_b: float32 [2048, 64], P(('ja', 'ia', 'ka')), may hold values from -60 to 60
- factor_c: float32 [8192, 64], P(('ka', 'ia', 'ja')), may hold values from -60 to 60
Outputs:
- grad_b: float32 [2048, 64], P(('ja', 'ia', 'ka'))
- grad_c: float32 [8192, 64], P(('ka', 'ia', 'ja'))
The draws below stay inside these ranges and needn't reach their ends.
All inputs are finite; a program needn't handle non-finite values.
Results may differ from the reference program's by a relative error of at most 0.0003.
Values sent between devices are 32-bit elements; how exact they have to be, the bound alone decides.
No kernel may reach another device: no remote copies, remote signals or barrier semaphores. Data moves between devices by JAX's collectives and lax.ppermute only.
A program may use at most 32 MiB of HBM per device.

```python
import jax
import jax.numpy as jnp
from jax import lax

RANK = 64
DIM_I = 16
DIM_J = 2048
DIM_K = 8192


def scale_table(key, count, width):
    key_row, key_col = jax.random.split(key, 2)
    position = jnp.arange(count, dtype=jnp.float32) / count
    row_scale = (0.5 + position) * 10.0 ** (jax.random.uniform(key_row, (count,), jnp.float32) - 0.5)
    col_scale = 10.0 ** (jax.random.uniform(key_col, (width,), jnp.float32) - 0.5)
    return row_scale[:, None] * col_scale[None, :]


def draw_factor_b(key, part):
    key = jax.random.fold_in(key, 11)
    key_value = jax.random.fold_in(key, 0)
    key_scale = jax.random.fold_in(key, 2)
    values = jax.random.truncated_normal(key_value, -4.0, 4.0, (DIM_J, RANK), jnp.float32)
    return (values * scale_table(key_scale, DIM_J, RANK)).astype(jnp.float32)


def draw_factor_c(key, part):
    key = jax.random.fold_in(key, 23)
    key_value = jax.random.fold_in(key, 0)
    key_scale = jax.random.fold_in(key, 2)
    values = jax.random.truncated_normal(key_value, -4.0, 4.0, (DIM_K, RANK), jnp.float32)
    return (values * scale_table(key_scale, DIM_K, RANK)).astype(jnp.float32)


def strengthened(result, key, source, target, shards_of, factor):
    owner, partner = [(jnp.arange(result.shape[axis_at]) // (result.shape[axis_at] // shards_of)).reshape([-1 if axis == axis_at else 1 for axis in range(result.ndim)]) for axis_at in (source, target)]
    chosen = jax.random.permutation(key, shards_of)[partner]
    strong = (owner == chosen) | (owner == (partner + shards_of // 2) % shards_of)
    return jnp.where(strong, factor * result, result)


def level_of(stream_key, dims, cuts, smallest, largest):
    def one(dim, blocks):
        heights = jax.random.uniform(jax.random.fold_in(jax.random.fold_in(stream_key, 6), dim), (blocks,), jnp.float32, smallest / len(cuts), largest / len(cuts))
        return jnp.repeat(jnp.exp(heights), dims[dim] // blocks).reshape((-1,) + (1,) * (len(dims) - dim - 1))

    level = one(*cuts[0])
    for cut in cuts[1:]:
        level = level * one(*cut)
    return level


def normal_values(key, dims, deviation, reach, shards=(), kind=jnp.bfloat16):
    entries = deviation * jax.random.normal(key, dims, jnp.float32)
    if shards:
        entries = entries * level_of(key, dims, shards, -0.22, 0.18)
    return jnp.clip(entries, -reach, reach).astype(kind)


def bell_draw_with(key, extent, deviation, limit, pieces, heavy, kind=jnp.bfloat16):
    drawn = deviation * jax.random.normal(key, extent, jnp.float32)
    if pieces:
        drawn = drawn * level_of(key, extent, pieces, -0.22, 0.18)
    return jnp.clip(strengthened(drawn, jax.random.fold_in(key, 3), *heavy), -limit, limit).astype(kind)


def setup_inputs(seed: int = 0) -> dict:
    keys = jax.random.split(jax.random.key(seed), 5)
    return {
        "tensor": bell_draw_with(keys[0], (DIM_I, DIM_J, DIM_K), 1.0, 6.0, ((0, 4), (1, 8), (2, 32)), (2, 1, 32, 2.75), jnp.float32),
        "factor_a": normal_values(keys[1], (DIM_I, RANK), (DIM_I * DIM_J) ** -0.5, 0.03125, (), jnp.float32),
        "factor_b": draw_factor_b(jax.random.fold_in(keys[4], 71), 0),
        "factor_c": draw_factor_c(jax.random.fold_in(keys[4], 71), 0),
    }


def gram_matrix(matrix):
    return jnp.dot(matrix.T, matrix, precision=lax.Precision.HIGHEST, preferred_element_type=jnp.float32)


def reference(tensor, factor_a, factor_b, factor_c):
    flat = tensor.reshape(DIM_I * DIM_J, DIM_K)
    inner = jnp.dot(flat, factor_c, precision=lax.Precision.HIGHEST, preferred_element_type=jnp.float32)
    inner = inner.reshape(DIM_I, DIM_J, RANK)
    mttkrp_b = jnp.einsum("ijr,ir->jr", inner, factor_a, precision=lax.Precision.HIGHEST)
    weights = (factor_a[:, None, :] * factor_b[None, :, :]).reshape(DIM_I * DIM_J, RANK)
    mttkrp_c = lax.dot_general(flat, weights, (((0,), (0,)), ((), ())), precision=lax.Precision.HIGHEST, preferred_element_type=jnp.float32)
    gram_a = gram_matrix(factor_a)
    gram_b = gram_matrix(factor_b)
    gram_c = gram_matrix(factor_c)
    grad_b = jnp.dot(factor_b, gram_a * gram_c, precision=lax.Precision.HIGHEST, preferred_element_type=jnp.float32) - mttkrp_b
    grad_c = jnp.dot(factor_c, gram_a * gram_b, precision=lax.Precision.HIGHEST, preferred_element_type=jnp.float32) - mttkrp_c
    return grad_b, grad_c
```

```python
import jax
import jax.numpy as jnp
from jax import lax
from jax.experimental import pallas as pl
from jax.experimental.pallas import tpu as pltpu
from jax.sharding import PartitionSpec as P

F32 = jnp.float32
BF16 = jnp.bfloat16
VMEM = pl.BlockSpec(memory_space=pltpu.VMEM)

NI, NJ, NK = 4, 8, 32
NP = NI * NJ
R = 64
ROWS = 256
M1, M2, M3 = 5, 9, 6


def coords():
    return lax.axis_index("ia"), lax.axis_index("ja")


def split(x):
    hi = x.astype(BF16)
    return hi, (x - hi.astype(F32)).astype(BF16)


def dot(x, y):
    return jnp.dot(x, y, preferred_element_type=F32)


def dot_exact(x, y, dims):
    return lax.dot_general(
        x, y, (dims, ((), ())), precision=lax.Precision.HIGHEST, preferred_element_type=F32
    )


def pack_kernel(b_ref, c_ref, out_ref):
    for q in range(4):
        row = jnp.concatenate([c_ref[q : q + 1, :], c_ref[q + 4 : q + 5, :]], axis=1)
        out_ref[pl.ds(q, NP, stride=M1), :] = jnp.broadcast_to(row, (NP, 2 * R))
    row = jnp.concatenate([b_ref[0:1, :], b_ref[1:2, :]], axis=1)
    out_ref[pl.ds(4, NP, stride=M1), :] = jnp.broadcast_to(row, (NP, 2 * R))


def second_kernel(t_ref, a_ref, r1_ref, out_ref, c_ref, sec_ref, gram_ref):
    ia, ja = coords()
    for q in range(4):
        rows = r1_ref[pl.ds(q, NP, stride=M1), :]
        c_ref[pl.ds(q, NP, stride=8), :] = rows[:, :R]
        c_ref[pl.ds(q + 4, NP, stride=8), :] = rows[:, R:]
    c = c_ref[...]
    second = None
    for i in range(NI):
        w_hi, w_lo = split(c * a_ref[pl.ds(NI * ia + i, 1), :])
        t_hi, t_lo = split(t_ref[i])
        part = dot(t_hi, w_hi) + (dot(t_hi, w_lo) + dot(t_lo, w_hi))
        second = part if second is None else second + part
    sec_ref[...] = second
    gram_ref[...] = dot_exact(c, c, ((0,), (0,)))
    p = ia * NJ + ja
    for i in range(NI):
        row = r1_ref[pl.ds((i * NJ + ja) * M1 + 4, 1), :]
        out_ref[pl.ds(i, NK, stride=M2), :] = jnp.broadcast_to(row, (NK, 2 * R))
        even = sec_ref[pl.ds(i * 2 * NK, NK, stride=2), :]
        odd = sec_ref[pl.ds(i * 2 * NK + 1, NK, stride=2), :]
        out_ref[pl.ds(4 + i, NK, stride=M2), :] = jnp.concatenate([even, odd], axis=1)
    row = jnp.concatenate([gram_ref[pl.ds(2 * p, 1), :], gram_ref[pl.ds(2 * p + 1, 1), :]], axis=1)
    out_ref[pl.ds(8, NK, stride=M2), :] = jnp.broadcast_to(row, (NK, 2 * R))


def third_kernel(t_ref, a_ref, c_ref, r2_ref, out_ref, b_ref, third_ref):
    ia, _ = coords()
    for i in range(NI):
        rows = r2_ref[pl.ds(i, NK, stride=M2), :]
        b_ref[pl.ds(i * 2 * NK, NK, stride=2), :] = rows[:, :R]
        b_ref[pl.ds(i * 2 * NK + 1, NK, stride=2), :] = rows[:, R:]
    b = b_ref[...]
    a = a_ref[pl.ds(NI * ia, NI), :]
    third = None
    for h in range(NI // 2):
        pair = jnp.concatenate([b * a[2 * h : 2 * h + 1, :], b * a[2 * h + 1 : 2 * h + 2, :]], axis=1)
        w_hi, w_lo = split(pair.T)
        for e in range(2):
            t_hi, t_lo = split(t_ref[2 * h + e])
            x_hi, x_lo = w_hi[e * R : (e + 1) * R, :], w_lo[e * R : (e + 1) * R, :]
            part = dot(x_hi, t_hi) + (dot(x_lo, t_hi) + dot(x_hi, t_lo))
            third = part if third is None else third + part
    gram_b = dot_exact(b, b, ((0,), (0,)))
    gram_a = dot_exact(a, a, ((0,), (0,)))
    third_ref[...] = dot_exact(c_ref[...], gram_a * gram_b, ((1,), (0,))) - third.T
    for q in range(4):
        left = third_ref[pl.ds(q, NP, stride=8), :]
        right = third_ref[pl.ds(q + 4, NP, stride=8), :]
        out_ref[pl.ds(q, NP, stride=M3), :] = jnp.concatenate([left, right], axis=1)
    for i in range(NI):
        row = jnp.sum(r2_ref[pl.ds(4 + i, NK, stride=M2), :], axis=0, keepdims=True)
        out_ref[pl.ds(i * NJ * M3 + 4, NJ, stride=M3), :] = jnp.broadcast_to(row, (NJ, 2 * R))
    row = jnp.sum(r2_ref[pl.ds(8, NK, stride=M2), :], axis=0, keepdims=True)
    out_ref[pl.ds(5, NP, stride=M3), :] = jnp.broadcast_to(row, (NP, 2 * R))


def final_kernel(a_ref, b_ref, r3_ref, gb_ref, gc_ref, gram_ref):
    _, ja = coords()
    for q in range(4):
        row = jnp.sum(r3_ref[pl.ds(q, NP, stride=M3), :], axis=0, keepdims=True)
        gc_ref[q : q + 1, :] = row[:, :R]
        gc_ref[q + 4 : q + 5, :] = row[:, R:]
    rows = r3_ref[pl.ds(5, NP, stride=M3), :]
    gram_ref[pl.ds(0, NP, stride=2), :] = rows[:, :R]
    gram_ref[pl.ds(1, NP, stride=2), :] = rows[:, R:]
    a = a_ref[...]
    gram_a = dot_exact(a, a, ((0,), (0,)))
    b = jnp.concatenate([b_ref[...], jnp.zeros((6, R), F32)], axis=0)
    gb = dot_exact(b, gram_a * gram_ref[...], ((1,), (0,)))
    row = r3_ref[pl.ds(ja * M3 + 4, 1), :]
    for i in range(1, NI):
        row = row + r3_ref[pl.ds((i * NJ + ja) * M3 + 4, 1), :]
    gb_ref[0:1, :] = gb[0:1, :] - row[:, :R]
    gb_ref[1:2, :] = gb[1:2, :] - row[:, R:]


def call(kernel, outs, operands, scratch=()):
    return pl.pallas_call(
        kernel,
        out_shape=[jax.ShapeDtypeStruct(shape, F32) for shape in outs],
        in_specs=[VMEM] * len(operands),
        out_specs=[VMEM] * len(outs),
        scratch_shapes=[pltpu.VMEM(shape, F32) for shape in scratch],
        compiler_params=pltpu.CompilerParams(vmem_limit_bytes=16 * 1024 * 1024),
    )(*operands)


def exchange(x, axes, rows):
    peers = x.shape[0] // rows
    x = x.reshape(peers, rows, 1, 2 * R)
    x = lax.all_to_all(x, axes, 0, 0)
    return x.reshape(peers * rows, 2 * R)


def per_device(tensor, factor_a, factor_b, factor_c):
    (s1,) = call(pack_kernel, [(NP * M1, 2 * R)], (factor_b, factor_c))
    r1 = exchange(s1, ("ia", "ja"), M1)
    s2, c = call(
        second_kernel,
        [(NK * M2, 2 * R), (ROWS, R)],
        (tensor, factor_a, r1),
        [(ROWS, R), (R, R)],
    )
    r2 = exchange(s2, "ka", M2)
    (s3,) = call(
        third_kernel,
        [(NP * M3, 2 * R)],
        (tensor, factor_a, c, r2),
        [(ROWS, R), (ROWS, R)],
    )
    r3 = exchange(s3, ("ia", "ja"), M3)
    gb, gc = call(final_kernel, [(2, R), (8, R)], (factor_a, factor_b, r3), [(R, R)])
    return gb, gc


def solution(mesh):
    placed = (P("ia", "ja", "ka"), P(), P(("ja", "ia", "ka"), None), P(("ka", "ia", "ja"), None))
    return jax.shard_map(
        per_device,
        mesh=mesh,
        in_specs=placed,
        out_specs=(P(("ja", "ia", "ka"), None), P(("ka", "ia", "ja"), None)),
        check_vma=False,
    )
```

```python
import jax
import jax.numpy as jnp
from jax import lax
from jax.experimental import pallas as pl
from jax.experimental.pallas import tpu as pltpu
from jax.sharding import PartitionSpec as P

F32 = jnp.float32
BF16 = jnp.bfloat16
VMEM = pl.BlockSpec(memory_space=pltpu.VMEM)
HBM = pl.BlockSpec(memory_space=pltpu.HBM)

NI, NJ, NK = 4, 8, 32
NP = NI * NJ
R = 64
ROWS = 256
M1, M2, M3 = 5, 9, 5


def coords():
    return lax.axis_index("ia"), lax.axis_index("ja")


def split(x):
    hi = x.astype(BF16)
    return hi, (x - hi.astype(F32)).astype(BF16)


def dot(x, y):
    return jnp.dot(x, y, preferred_element_type=F32)


def dot_exact(x, y, dims):
    return lax.dot_general(
        x, y, (dims, ((), ())), precision=lax.Precision.HIGHEST, preferred_element_type=F32
    )


def fetch(source, target, sem):
    copy = pltpu.make_async_copy(source, target, sem)
    copy.start()
    return copy


def pack_kernel(b_hbm, c_hbm, t_hbm, out_ref, t_ref, b_ref, c_ref, sems):
    copies = [fetch(b_hbm, b_ref, sems.at[0]), fetch(c_hbm, c_ref, sems.at[1])]
    block = fetch(t_hbm, t_ref, sems.at[2])
    for copy in copies:
        copy.wait()
    for q in range(4):
        row = jnp.concatenate([c_ref[q : q + 1, :], c_ref[q + 4 : q + 5, :]], axis=1)
        out_ref[pl.ds(q, NP, stride=M1), :] = jnp.broadcast_to(row, (NP, 2 * R))
    row = jnp.concatenate([b_ref[0:1, :], b_ref[1:2, :]], axis=1)
    out_ref[pl.ds(4, NP, stride=M1), :] = jnp.broadcast_to(row, (NP, 2 * R))
    block.wait()


def second_kernel(t_ref, a_ref, r1_ref, out_ref, c_ref, sec_ref, gram_ref):
    ia, ja = coords()
    p = ia * NJ + ja
    for q in range(4):
        rows = r1_ref[pl.ds(q, NP, stride=M1), :]
        c_ref[pl.ds(q, NP, stride=8), :] = rows[:, :R]
        c_ref[pl.ds(q + 4, NP, stride=8), :] = rows[:, R:]
    c = c_ref[...]
    a = a_ref[...]
    gram_a = dot_exact(a, a, ((0,), (0,)))
    gram_ref[...] = gram_a * dot_exact(c, c, ((0,), (0,)))
    row = jnp.concatenate([gram_ref[pl.ds(2 * p, 1), :], gram_ref[pl.ds(2 * p + 1, 1), :]], axis=1)
    out_ref[pl.ds(8, NK, stride=M2), :] = jnp.broadcast_to(row, (NK, 2 * R))
    for i in range(NI):
        row = r1_ref[pl.ds((i * NJ + ja) * M1 + 4, 1), :]
        out_ref[pl.ds(i, NK, stride=M2), :] = jnp.broadcast_to(row, (NK, 2 * R))
    weights = [split(c * a_ref[pl.ds(NI * ia + i, 1), :]) for i in range(NI)]
    second = None
    for i in range(NI):
        w_hi, w_lo = weights[i]
        t_hi, t_lo = split(t_ref[i])
        part = dot(t_hi, w_hi) + (dot(t_hi, w_lo) + dot(t_lo, w_hi))
        second = part if second is None else second + part
    sec_ref[...] = second
    for i in range(NI):
        even = sec_ref[pl.ds(i * 2 * NK, NK, stride=2), :]
        odd = sec_ref[pl.ds(i * 2 * NK + 1, NK, stride=2), :]
        out_ref[pl.ds(4 + i, NK, stride=M2), :] = jnp.concatenate([even, odd], axis=1)


def third_kernel(t_ref, a_ref, c_ref, r1_ref, r2_ref, out_ref, b_ref, third_ref):
    ia, ja = coords()
    p = ia * NJ + ja
    for i in range(NI):
        rows = r2_ref[pl.ds(i, NK, stride=M2), :]
        b_ref[pl.ds(i * 2 * NK, NK, stride=2), :] = rows[:, :R]
        b_ref[pl.ds(i * 2 * NK + 1, NK, stride=2), :] = rows[:, R:]
    b = b_ref[...]
    a = a_ref[pl.ds(NI * ia, NI), :]
    gram_b = dot_exact(b, b, ((0,), (0,)))
    gram_a = dot_exact(a, a, ((0,), (0,)))
    row = jnp.sum(r2_ref[pl.ds(8, NK, stride=M2), :], axis=0, keepdims=True)
    place = lax.broadcasted_iota(jnp.int32, (R, R), 0)
    gram = jnp.where(place == 2 * p, row[:, :R], jnp.where(place == 2 * p + 1, row[:, R:], 0.0))
    rows = r1_ref[pl.ds(4, NP, stride=M1), :]
    grad_b = dot_exact(jnp.concatenate([rows[:, :R], rows[:, R:]], axis=0), gram, ((1,), (0,)))
    grad_b = jnp.concatenate([grad_b[:NP, :], grad_b[NP:, :]], axis=1)
    summed = jnp.concatenate(
        [
            jnp.broadcast_to(
                jnp.sum(r2_ref[pl.ds(4 + i, NK, stride=M2), :], axis=0, keepdims=True), (NJ, 2 * R)
            )
            for i in range(NI)
        ],
        axis=0,
    )
    peer = lax.broadcasted_iota(jnp.int32, (NP, 2 * R), 0)
    grad_b = grad_b - jnp.where(lax.rem(peer, NJ) == ja, summed, 0.0)
    out_ref[pl.ds(4, NP, stride=M3), :] = grad_b
    third = None
    for h in range(NI // 2):
        pair = jnp.concatenate([b * a[2 * h : 2 * h + 1, :], b * a[2 * h + 1 : 2 * h + 2, :]], axis=1)
        w_hi, w_lo = split(pair.T)
        for e in range(2):
            t_hi, t_lo = split(t_ref[2 * h + e])
            x_hi, x_lo = w_hi[e * R : (e + 1) * R, :], w_lo[e * R : (e + 1) * R, :]
            part = dot(x_hi, t_hi) + (dot(x_lo, t_hi) + dot(x_hi, t_lo))
            third = part if third is None else third + part
    third_ref[...] = dot_exact(c_ref[...], gram_a * gram_b, ((1,), (0,))) - third.T
    for q in range(4):
        left = third_ref[pl.ds(q, NP, stride=8), :]
        right = third_ref[pl.ds(q + 4, NP, stride=8), :]
        out_ref[pl.ds(q, NP, stride=M3), :] = jnp.concatenate([left, right], axis=1)


def final_kernel(r3_ref, gb_ref, gc_ref):
    for q in range(4):
        row = jnp.sum(r3_ref[pl.ds(q, NP, stride=M3), :], axis=0, keepdims=True)
        gc_ref[q : q + 1, :] = row[:, :R]
        gc_ref[q + 4 : q + 5, :] = row[:, R:]
    row = jnp.sum(r3_ref[pl.ds(4, NP, stride=M3), :], axis=0, keepdims=True)
    gb_ref[0:1, :] = row[:, :R]
    gb_ref[1:2, :] = row[:, R:]


def call(kernel, outs, operands, scratch=(), copies=0, in_hbm=0):
    scratch_shapes = [pltpu.VMEM(shape, F32) for shape in scratch]
    if copies:
        scratch_shapes.append(pltpu.SemaphoreType.DMA((copies,)))
    return pl.pallas_call(
        kernel,
        out_shape=[jax.ShapeDtypeStruct(shape, F32) for shape in outs],
        in_specs=[HBM] * in_hbm + [VMEM] * (len(operands) - in_hbm),
        out_specs=[VMEM] * len(outs),
        scratch_shapes=scratch_shapes,
        compiler_params=pltpu.CompilerParams(vmem_limit_bytes=16 * 1024 * 1024),
    )(*[pltpu.with_memory_space_constraint(x, pltpu.HBM) for x in operands[:in_hbm]], *operands[in_hbm:])


def exchange(x, axes, rows):
    peers = x.shape[0] // rows
    x = x.reshape(peers, rows, 1, 2 * R)
    x = lax.all_to_all(x, axes, 0, 0)
    return x.reshape(peers * rows, 2 * R)


def per_device(tensor, factor_a, factor_b, factor_c):
    s1, block = call(
        pack_kernel,
        [(NP * M1, 2 * R), tensor.shape],
        (factor_b, factor_c, tensor),
        [(2, R), (8, R)],
        copies=3,
        in_hbm=3,
    )
    r1 = exchange(s1, ("ia", "ja"), M1)
    s2, c = call(
        second_kernel,
        [(NK * M2, 2 * R), (ROWS, R)],
        (block, factor_a, r1),
        [(ROWS, R), (R, R)],
    )
    r2 = exchange(s2, "ka", M2)
    (s3,) = call(
        third_kernel,
        [(NP * M3, 2 * R)],
        (block, factor_a, c, r1, r2),
        [(ROWS, R), (ROWS, R)],
    )
    r3 = exchange(s3, ("ia", "ja"), M3)
    return tuple(call(final_kernel, [(2, R), (8, R)], (r3,)))


def solution(mesh):
    placed = (P("ia", "ja", "ka"), P(), P(("ja", "ia", "ka"), None), P(("ka", "ia", "ja"), None))
    return jax.shard_map(
        per_device,
        mesh=mesh,
        in_specs=placed,
        out_specs=(P(("ja", "ia", "ka"), None), P(("ka", "ia", "ja"), None)),
        check_vma=False,
    )
```

```python
import jax
import jax.numpy as jnp
from jax import lax
from jax.experimental import pallas as pl
from jax.experimental.pallas import tpu as pltpu
from jax.sharding import PartitionSpec as P

F32 = jnp.float32
BF16 = jnp.bfloat16
VMEM = pl.BlockSpec(memory_space=pltpu.VMEM)
HBM = pl.BlockSpec(memory_space=pltpu.HBM)

NI, NJ, NK = 4, 8, 32
NP = NI * NJ
R = 64
W = 2 * R
ROWS = 256
M1, M2, M3 = 5, 9, 5


def coords():
    return lax.axis_index("ia"), lax.axis_index("ja")


def rough(x):
    return x.astype(BF16).astype(F32)


def dot(x, y, dims=((1,), (0,))):
    return lax.dot_general(x, y, (dims, ((), ())), preferred_element_type=F32)


def dot_exact(x, y, dims):
    return lax.dot_general(
        x, y, (dims, ((), ())), precision=lax.Precision.HIGHEST, preferred_element_type=F32
    )


def left_half(x):
    return lax.broadcasted_iota(jnp.int32, x.shape, 1) < R


def join(x, y):
    return jnp.where(left_half(x), x, y)


def turned(x):
    return pltpu.roll(x, R, 1)


def twice(x):
    return x + turned(x)


def parts(x):
    return join(x, x - rough(x)).astype(BF16)


def split(x):
    hi = rough(x)
    return x.astype(BF16), (x - hi).astype(BF16)


def fetch(source, target, sem):
    copy = pltpu.make_async_copy(source, target, sem)
    copy.start()
    return copy


def pack_kernel(b_hbm, c_hbm, t_hbm, out_ref, t_ref, b_ref, c_ref, sems):
    block = fetch(t_hbm, t_ref, sems.at[2])
    copies = [fetch(b_hbm, b_ref, sems.at[0]), fetch(c_hbm, c_ref, sems.at[1])]
    for copy in copies:
        copy.wait()
    for q in range(4):
        row = jnp.concatenate([c_ref[q : q + 1, :], c_ref[q + 4 : q + 5, :]], axis=1)
        out_ref[pl.ds(q, NP, stride=M1), :] = jnp.broadcast_to(row, (NP, W))
    row = jnp.concatenate([b_ref[0:1, :], b_ref[1:2, :]], axis=1)
    out_ref[pl.ds(4, NP, stride=M1), :] = jnp.broadcast_to(row, (NP, W))
    block.wait()


def second_kernel(t_ref, a_ref, r1_ref, out_ref, cc_ref, c_ref, sec_ref, gram_ref):
    ia, ja = coords()
    p = ia * NJ + ja
    for q in range(4):
        rows = r1_ref[pl.ds(q, NP, stride=M1), :]
        other = turned(rows)
        c_ref[pl.ds(q, NP, stride=8), :] = join(rows, other)
        c_ref[pl.ds(q + 4, NP, stride=8), :] = join(other, rows)
    c = c_ref[...]
    a = a_ref[...]
    aa = jnp.concatenate([a, a], axis=1)
    cc = parts(c)
    cc_ref[...] = cc
    gram_a = dot_exact(a, aa, ((0,), (0,)))
    gram_c = dot(cc, cc, ((0,), (0,)))
    gram_ref[...] = gram_a * twice(gram_c[:R, :] + gram_c[R:, :])
    sec_ref[...] = aa
    weights = [parts(c * sec_ref[pl.ds(NI * ia + i, 1), :]) for i in range(NI)]
    second = None
    for i in range(NI):
        t_hi, t_lo = split(t_ref[i])
        part = dot(t_hi, weights[i]) + dot(t_lo, weights[i])
        second = part if second is None else second + part
    row = join(gram_ref[pl.ds(2 * p, 1), :], gram_ref[pl.ds(2 * p + 1, 1), :])
    out_ref[pl.ds(8, NK, stride=M2), :] = jnp.broadcast_to(row, (NK, W))
    for i in range(NI):
        row = r1_ref[pl.ds((i * NJ + ja) * M1 + 4, 1), :]
        out_ref[pl.ds(i, NK, stride=M2), :] = jnp.broadcast_to(row, (NK, W))
    c_ref[...] = second
    for i in range(NI):
        even = c_ref[pl.ds(i * 2 * NK, NK, stride=2), :]
        odd = c_ref[pl.ds(i * 2 * NK + 1, NK, stride=2), :]
        out_ref[pl.ds(4 + i, NK, stride=M2), :] = join(twice(even), twice(odd))


def third_kernel(t_ref, a_ref, cc_ref, r1_ref, r2_ref, out_ref, b_ref, third_ref):
    ia, ja = coords()
    p = ia * NJ + ja
    for i in range(NI):
        rows = r2_ref[pl.ds(i, NK, stride=M2), :]
        other = turned(rows)
        b_ref[pl.ds(i * 2 * NK, NK, stride=2), :] = join(rows, other)
        b_ref[pl.ds(i * 2 * NK + 1, NK, stride=2), :] = join(other, rows)
    b = b_ref[...]
    a = a_ref[pl.ds(NI * ia, NI), :]
    aa = jnp.concatenate([a, a], axis=1)
    a_turned = jnp.concatenate([aa, aa], axis=0).T[:R, :]
    bt = b.T[:R, :]
    third = None
    for i in range(NI):
        x = jnp.concatenate(split(bt * a_turned[:, i : i + 1]), axis=0)
        t_hi, t_lo = split(t_ref[i])
        part = dot(x, t_hi) + dot(x, t_lo)
        third = part if third is None else third + part
    gram_b = dot(jnp.concatenate(split(bt), axis=0), parts(b))
    gram_b = twice(gram_b[:R, :] + gram_b[R:, :])
    gram_a = a_turned[:, 0:1] * aa[0:1, :]
    for i in range(1, NI):
        gram_a = gram_a + a_turned[:, i : i + 1] * aa[i : i + 1, :]
    gram = parts(gram_a * gram_b)
    row = jnp.sum(r2_ref[pl.ds(8, NK, stride=M2), :], axis=0, keepdims=True)
    place = lax.broadcasted_iota(jnp.int32, (R, R), 0)
    mine = jnp.where(place == 2 * p, row[:, :R], jnp.where(place == 2 * p + 1, row[:, R:], 0.0))
    rows = r1_ref[pl.ds(4, NP, stride=M1), :]
    grad_b = dot_exact(jnp.concatenate([rows[:, :R], rows[:, R:]], axis=0), mine, ((1,), (0,)))
    grad_b = jnp.concatenate([grad_b[:NP, :], grad_b[NP:, :]], axis=1)
    summed = jnp.concatenate(
        [
            jnp.broadcast_to(
                jnp.sum(r2_ref[pl.ds(4 + i, NK, stride=M2), :], axis=0, keepdims=True), (NJ, W)
            )
            for i in range(NI)
        ],
        axis=0,
    )
    peer = lax.broadcasted_iota(jnp.int32, (NP, W), 0)
    grad_b = grad_b - jnp.where(lax.rem(peer, NJ) == ja, summed, 0.0)
    out_ref[pl.ds(4, NP, stride=M3), :] = grad_b
    third_ref[...] = twice(dot(cc_ref[...], jnp.concatenate([gram, gram], axis=0)) - third.T)
    for q in range(4):
        left = third_ref[pl.ds(q, NP, stride=8), :]
        right = third_ref[pl.ds(q + 4, NP, stride=8), :]
        out_ref[pl.ds(q, NP, stride=M3), :] = join(left, right)


def final_kernel(r3_ref, gb_ref, gc_ref):
    for q in range(4):
        row = jnp.sum(r3_ref[pl.ds(q, NP, stride=M3), :], axis=0, keepdims=True)
        gc_ref[q : q + 1, :] = row[:, :R]
        gc_ref[q + 4 : q + 5, :] = row[:, R:]
    row = jnp.sum(r3_ref[pl.ds(4, NP, stride=M3), :], axis=0, keepdims=True)
    gb_ref[0:1, :] = row[:, :R]
    gb_ref[1:2, :] = row[:, R:]


def call(kernel, outs, operands, scratch=(), copies=0, in_hbm=0, kinds=None):
    kinds = kinds or [F32] * len(outs)
    scratch_shapes = [pltpu.VMEM(shape, F32) for shape in scratch]
    if copies:
        scratch_shapes.append(pltpu.SemaphoreType.DMA((copies,)))
    return pl.pallas_call(
        kernel,
        out_shape=[jax.ShapeDtypeStruct(shape, kind) for shape, kind in zip(outs, kinds)],
        in_specs=[HBM] * in_hbm + [VMEM] * (len(operands) - in_hbm),
        out_specs=[VMEM] * len(outs),
        scratch_shapes=scratch_shapes,
        compiler_params=pltpu.CompilerParams(vmem_limit_bytes=16 * 1024 * 1024),
    )(*[pltpu.with_memory_space_constraint(x, pltpu.HBM) for x in operands[:in_hbm]], *operands[in_hbm:])


def exchange(x, axes, rows):
    peers = x.shape[0] // rows
    x = x.reshape(peers, rows, 1, W)
    x = lax.all_to_all(x, axes, 0, 0)
    return x.reshape(peers * rows, W)


def per_device(tensor, factor_a, factor_b, factor_c):
    s1, block = call(
        pack_kernel,
        [(NP * M1, W), tensor.shape],
        (factor_b, factor_c, tensor),
        [(2, R), (8, R)],
        copies=3,
        in_hbm=3,
    )
    r1 = exchange(s1, ("ia", "ja"), M1)
    s2, cc = call(
        second_kernel,
        [(NK * M2, W), (ROWS, W)],
        (block, factor_a, r1),
        [(ROWS, W), (16, W), (R, W)],
        kinds=[F32, BF16],
    )
    r2 = exchange(s2, "ka", M2)
    (s3,) = call(
        third_kernel,
        [(NP * M3, W)],
        (block, factor_a, cc, r1, r2),
        [(ROWS, W), (ROWS, W)],
    )
    r3 = exchange(s3, ("ia", "ja"), M3)
    return tuple(call(final_kernel, [(2, R), (8, R)], (r3,)))


def solution(mesh):
    placed = (P("ia", "ja", "ka"), P(), P(("ja", "ia", "ka"), None), P(("ka", "ia", "ja"), None))
    return jax.shard_map(
        per_device,
        mesh=mesh,
        in_specs=placed,
        out_specs=(P(("ja", "ia", "ka"), None), P(("ka", "ia", "ja"), None)),
        check_vma=False,
    )
```

```python
import jax
import jax.numpy as jnp
from jax import lax
from jax.experimental import pallas as pl
from jax.experimental.pallas import tpu as pltpu
from jax.sharding import PartitionSpec as P

F32 = jnp.float32
BF16 = jnp.bfloat16
VMEM = pl.BlockSpec(memory_space=pltpu.VMEM)
HBM = pl.BlockSpec(memory_space=pltpu.HBM)

NI, NJ, NK = 4, 8, 32
NP = NI * NJ
R = 64
W = 2 * R
ROWS = 256
M1, M2, M3 = 5, 9, 5


def coords():
    return lax.axis_index("ia"), lax.axis_index("ja")


def rough(x):
    return x.astype(BF16).astype(F32)


def dot(x, y, dims=((1,), (0,))):
    return lax.dot_general(x, y, (dims, ((), ())), preferred_element_type=F32)


def dot_exact(x, y, dims):
    return lax.dot_general(
        x, y, (dims, ((), ())), precision=lax.Precision.HIGHEST, preferred_element_type=F32
    )


def left_half(x):
    return lax.broadcasted_iota(jnp.int32, x.shape, 1) < R


def join(x, y):
    return jnp.where(left_half(x), x, y)


def turned(x):
    return pltpu.roll(x, R, 1)


def twice(x):
    return x + turned(x)


def parts(x):
    return join(x, x - rough(x)).astype(BF16)


def split(x):
    hi = rough(x)
    return x.astype(BF16), (x - hi).astype(BF16)


def fetch(source, target, sem):
    copy = pltpu.make_async_copy(source, target, sem)
    copy.start()
    return copy


def pack_kernel(b_hbm, c_hbm, out_ref, b_ref, c_ref, sems):
    copies = [fetch(b_hbm, b_ref, sems.at[0]), fetch(c_hbm, c_ref, sems.at[1])]
    for copy in copies:
        copy.wait()
    for q in range(4):
        row = jnp.concatenate([c_ref[q : q + 1, :], c_ref[q + 4 : q + 5, :]], axis=1)
        out_ref[pl.ds(q, NP, stride=M1), :] = jnp.broadcast_to(row, (NP, W))
    row = jnp.concatenate([b_ref[0:1, :], b_ref[1:2, :]], axis=1)
    out_ref[pl.ds(4, NP, stride=M1), :] = jnp.broadcast_to(row, (NP, W))


def second_kernel(t_ref, a_ref, r1_ref, out_ref, cc_ref, c_ref, sec_ref, gram_ref):
    ia, ja = coords()
    p = ia * NJ + ja
    for q in range(4):
        rows = r1_ref[pl.ds(q, NP, stride=M1), :]
        other = turned(rows)
        c_ref[pl.ds(q, NP, stride=8), :] = join(rows, other)
        c_ref[pl.ds(q + 4, NP, stride=8), :] = join(other, rows)
    c = c_ref[...]
    a = a_ref[...]
    aa = jnp.concatenate([a, a], axis=1)
    cc = parts(c)
    cc_ref[...] = cc
    gram_a = dot_exact(a, aa, ((0,), (0,)))
    gram_c = dot(cc, cc, ((0,), (0,)))
    gram_ref[...] = gram_a * twice(gram_c[:R, :] + gram_c[R:, :])
    sec_ref[...] = aa
    weights = [parts(c * sec_ref[pl.ds(NI * ia + i, 1), :]) for i in range(NI)]
    second = None
    for i in range(NI):
        t_hi, t_lo = split(t_ref[i])
        part = dot(t_hi, weights[i]) + dot(t_lo, weights[i])
        second = part if second is None else second + part
    row = join(gram_ref[pl.ds(2 * p, 1), :], gram_ref[pl.ds(2 * p + 1, 1), :])
    out_ref[pl.ds(8, NK, stride=M2), :] = jnp.broadcast_to(row, (NK, W))
    for i in range(NI):
        row = r1_ref[pl.ds((i * NJ + ja) * M1 + 4, 1), :]
        out_ref[pl.ds(i, NK, stride=M2), :] = jnp.broadcast_to(row, (NK, W))
    c_ref[...] = second
    for i in range(NI):
        even = c_ref[pl.ds(i * 2 * NK, NK, stride=2), :]
        odd = c_ref[pl.ds(i * 2 * NK + 1, NK, stride=2), :]
        out_ref[pl.ds(4 + i, NK, stride=M2), :] = join(twice(even), twice(odd))


def third_kernel(t_ref, a_ref, cc_ref, r1_ref, r2_ref, out_ref, b_ref, third_ref):
    ia, ja = coords()
    p = ia * NJ + ja
    for i in range(NI):
        rows = r2_ref[pl.ds(i, NK, stride=M2), :]
        other = turned(rows)
        b_ref[pl.ds(i * 2 * NK, NK, stride=2), :] = join(rows, other)
        b_ref[pl.ds(i * 2 * NK + 1, NK, stride=2), :] = join(other, rows)
    b = b_ref[...]
    a = a_ref[pl.ds(NI * ia, NI), :]
    aa = jnp.concatenate([a, a], axis=1)
    a_turned = jnp.concatenate([aa, aa], axis=0).T[:R, :]
    bt = b.T[:R, :]
    third = None
    for i in range(NI):
        x = jnp.concatenate(split(bt * a_turned[:, i : i + 1]), axis=0)
        t_hi, t_lo = split(t_ref[i])
        part = dot(x, t_hi) + dot(x, t_lo)
        third = part if third is None else third + part
    gram_b = dot(jnp.concatenate(split(bt), axis=0), parts(b))
    gram_b = twice(gram_b[:R, :] + gram_b[R:, :])
    gram_a = a_turned[:, 0:1] * aa[0:1, :]
    for i in range(1, NI):
        gram_a = gram_a + a_turned[:, i : i + 1] * aa[i : i + 1, :]
    gram = parts(gram_a * gram_b)
    row = jnp.sum(r2_ref[pl.ds(8, NK, stride=M2), :], axis=0, keepdims=True)
    place = lax.broadcasted_iota(jnp.int32, (R, R), 0)
    mine = jnp.where(place == 2 * p, row[:, :R], jnp.where(place == 2 * p + 1, row[:, R:], 0.0))
    rows = r1_ref[pl.ds(4, NP, stride=M1), :]
    grad_b = dot_exact(jnp.concatenate([rows[:, :R], rows[:, R:]], axis=0), mine, ((1,), (0,)))
    grad_b = jnp.concatenate([grad_b[:NP, :], grad_b[NP:, :]], axis=1)
    summed = jnp.concatenate(
        [
            jnp.broadcast_to(
                jnp.sum(r2_ref[pl.ds(4 + i, NK, stride=M2), :], axis=0, keepdims=True), (NJ, W)
            )
            for i in range(NI)
        ],
        axis=0,
    )
    peer = lax.broadcasted_iota(jnp.int32, (NP, W), 0)
    grad_b = grad_b - jnp.where(lax.rem(peer, NJ) == ja, summed, 0.0)
    out_ref[pl.ds(4, NP, stride=M3), :] = grad_b
    third_ref[...] = twice(dot(cc_ref[...], jnp.concatenate([gram, gram], axis=0)) - third.T)
    for q in range(4):
        left = third_ref[pl.ds(q, NP, stride=8), :]
        right = third_ref[pl.ds(q + 4, NP, stride=8), :]
        out_ref[pl.ds(q, NP, stride=M3), :] = join(left, right)


def final_kernel(r3_ref, gb_ref, gc_ref):
    for q in range(4):
        row = jnp.sum(r3_ref[pl.ds(q, NP, stride=M3), :], axis=0, keepdims=True)
        gc_ref[q : q + 1, :] = row[:, :R]
        gc_ref[q + 4 : q + 5, :] = row[:, R:]
    row = jnp.sum(r3_ref[pl.ds(4, NP, stride=M3), :], axis=0, keepdims=True)
    gb_ref[0:1, :] = row[:, :R]
    gb_ref[1:2, :] = row[:, R:]


def call(kernel, outs, operands, scratch=(), copies=0, in_hbm=0, kinds=None):
    kinds = kinds or [F32] * len(outs)
    scratch_shapes = [pltpu.VMEM(shape, F32) for shape in scratch]
    if copies:
        scratch_shapes.append(pltpu.SemaphoreType.DMA((copies,)))
    return pl.pallas_call(
        kernel,
        out_shape=[jax.ShapeDtypeStruct(shape, kind) for shape, kind in zip(outs, kinds)],
        in_specs=[HBM] * in_hbm + [VMEM] * (len(operands) - in_hbm),
        out_specs=[VMEM] * len(outs),
        scratch_shapes=scratch_shapes,
        compiler_params=pltpu.CompilerParams(vmem_limit_bytes=16 * 1024 * 1024),
        cost_estimate=pl.CostEstimate(flops=10**9, bytes_accessed=NP * M1 * W * 4, transcendentals=0),
    )(*[pltpu.with_memory_space_constraint(x, pltpu.HBM) for x in operands[:in_hbm]], *operands[in_hbm:])


def exchange(x, axes, rows):
    peers = x.shape[0] // rows
    x = x.reshape(peers, rows, 1, W)
    x = lax.all_to_all(x, axes, 0, 0)
    return x.reshape(peers * rows, W)


def per_device(tensor, factor_a, factor_b, factor_c):
    s1 = pl.pallas_call(
        pack_kernel,
        out_shape=pltpu.VMEM((NP * M1, W), F32),
        in_specs=[HBM] * 2,
        out_specs=VMEM,
        scratch_shapes=[
            pltpu.VMEM((2, R), F32),
            pltpu.VMEM((8, R), F32),
            pltpu.SemaphoreType.DMA((2,)),
        ],
        compiler_params=pltpu.CompilerParams(vmem_limit_bytes=16 * 1024 * 1024),
        cost_estimate=pl.CostEstimate(flops=10**9, bytes_accessed=NP * M1 * W * 4, transcendentals=0),
    )(*[pltpu.with_memory_space_constraint(x, pltpu.HBM) for x in (factor_b, factor_c)])
    block = tensor
    r1 = exchange(s1, ("ia", "ja"), M1)
    s2, cc = call(
        second_kernel,
        [(NK * M2, W), (ROWS, W)],
        (block, factor_a, r1),
        [(ROWS, W), (16, W), (R, W)],
        kinds=[F32, BF16],
    )
    r2 = exchange(s2, "ka", M2)
    (s3,) = call(
        third_kernel,
        [(NP * M3, W)],
        (block, factor_a, cc, r1, r2),
        [(ROWS, W), (ROWS, W)],
    )
    r3 = exchange(s3, ("ia", "ja"), M3)
    return tuple(call(final_kernel, [(2, R), (8, R)], (r3,)))


def solution(mesh):
    placed = (P("ia", "ja", "ka"), P(), P(("ja", "ia", "ka"), None), P(("ka", "ia", "ja"), None))
    return jax.shard_map(
        per_device,
        mesh=mesh,
        in_specs=placed,
        out_specs=(P(("ja", "ia", "ka"), None), P(("ka", "ia", "ja"), None)),
        check_vma=False,
    )
```

```python
import jax
import jax.numpy as jnp
from jax import lax
from jax.experimental import pallas as pl
from jax.experimental.pallas import tpu as pltpu
from jax.sharding import PartitionSpec as P

F32 = jnp.float32
BF16 = jnp.bfloat16
VMEM = pl.BlockSpec(memory_space=pltpu.VMEM)
HBM = pl.BlockSpec(memory_space=pltpu.HBM)

NI, NJ, NK = 4, 8, 32
NP = NI * NJ
R = 64
W = 2 * R
ROWS = 256
M1, M2, M3 = 5, 9, 5
HEAD_P, HEAD_K = 4, 30


def coords():
    return lax.axis_index("ia"), lax.axis_index("ja")


def rough(x):
    return x.astype(BF16).astype(F32)


def dot(x, y, dims=((1,), (0,))):
    return lax.dot_general(x, y, (dims, ((), ())), preferred_element_type=F32)


def dot_exact(x, y, dims):
    return lax.dot_general(
        x, y, (dims, ((), ())), precision=lax.Precision.HIGHEST, preferred_element_type=F32
    )


def left_half(x):
    return lax.broadcasted_iota(jnp.int32, x.shape, 1) < R


def join(x, y):
    return jnp.where(left_half(x), x, y)


def slot(p):
    return jnp.where(p == 0, HEAD_P, jnp.where(p == HEAD_P, 0, p))


def swapped(x):
    head = 8 * HEAD_P
    return jnp.concatenate([x[head : head + 8], x[8:head], x[:8], x[head + 8 :]], axis=0)


def turned(x):
    return pltpu.roll(x, R, 1)


def twice(x):
    return x + turned(x)


def parts(x):
    return join(x, x - rough(x)).astype(BF16)


def split(x):
    hi = rough(x)
    return x.astype(BF16), (x - hi).astype(BF16)


def fetch(source, target, sem):
    copy = pltpu.make_async_copy(source, target, sem)
    copy.start()
    return copy


def pack_kernel(b_hbm, c_hbm, out_ref, b_ref, c_ref, sems):
    copies = [fetch(b_hbm, b_ref, sems.at[0]), fetch(c_hbm, c_ref, sems.at[1])]
    for copy in copies:
        copy.wait()
    for q in range(4):
        row = jnp.concatenate([c_ref[q : q + 1, :], c_ref[q + 4 : q + 5, :]], axis=1)
        out_ref[pl.ds(q, NP, stride=M1), :] = jnp.broadcast_to(row, (NP, W))
    row = jnp.concatenate([b_ref[0:1, :], b_ref[1:2, :]], axis=1)
    out_ref[pl.ds(4, NP, stride=M1), :] = jnp.broadcast_to(row, (NP, W))


def second_kernel(t_ref, a_ref, r1_ref, out_ref, cc_ref, c_ref, sec_ref, gram_ref):
    ia, ja = coords()
    p = ia * NJ + ja
    for q in range(4):
        rows = r1_ref[pl.ds(q, NP, stride=M1), :]
        other = turned(rows)
        c_ref[pl.ds(q, NP, stride=8), :] = join(rows, other)
        c_ref[pl.ds(q + 4, NP, stride=8), :] = join(other, rows)
    c = swapped(c_ref[...])
    a = a_ref[...]
    aa = jnp.concatenate([a, a], axis=1)
    cc = parts(c)
    cc_ref[...] = cc
    gram_a = dot_exact(a, aa, ((0,), (0,)))
    gram_c = dot(cc, cc, ((0,), (0,)))
    gram_ref[...] = gram_a * twice(gram_c[:R, :] + gram_c[R:, :])
    sec_ref[...] = aa
    weights = [parts(c * sec_ref[pl.ds(NI * ia + i, 1), :]) for i in range(NI)]
    second = None
    for i in range(NI):
        t_hi, t_lo = split(t_ref[i])
        part = dot(t_hi, weights[i]) + dot(t_lo, weights[i])
        second = part if second is None else second + part
    row = join(gram_ref[pl.ds(2 * p, 1), :], gram_ref[pl.ds(2 * p + 1, 1), :])
    out_ref[pl.ds(8, NK, stride=M2), :] = jnp.broadcast_to(row, (NK, W))
    for i in range(NI):
        row = r1_ref[pl.ds(slot(i * NJ + ja) * M1 + 4, 1), :]
        out_ref[pl.ds(i, NK, stride=M2), :] = jnp.broadcast_to(row, (NK, W))
    c_ref[...] = second
    for i in range(NI):
        even = c_ref[pl.ds(i * 2 * NK, NK, stride=2), :]
        odd = c_ref[pl.ds(i * 2 * NK + 1, NK, stride=2), :]
        out_ref[pl.ds(4 + i, NK, stride=M2), :] = join(twice(even), twice(odd))
    head = HEAD_K * M2
    first, last = out_ref[4:8, :], out_ref[head + 4 : head + 8, :]
    out_ref[4:8, :] = last
    out_ref[head + 4 : head + 8, :] = first


def third_kernel(t_ref, a_ref, cc_ref, r1_ref, r2_ref, out_ref, b_ref, third_ref):
    ia, ja = coords()
    p = ia * NJ + ja
    for i in range(NI):
        rows = r2_ref[pl.ds(i, NK, stride=M2), :]
        other = turned(rows)
        b_ref[pl.ds(i * 2 * NK, NK, stride=2), :] = join(rows, other)
        b_ref[pl.ds(i * 2 * NK + 1, NK, stride=2), :] = join(other, rows)
        for ka, place in ((0, HEAD_K), (HEAD_K, 0)):
            row = r2_ref[place * M2 + i : place * M2 + i + 1, :]
            start = i * 2 * NK + 2 * ka
            b_ref[start : start + 1, :] = join(row, turned(row))
            b_ref[start + 1 : start + 2, :] = join(turned(row), row)
    b = b_ref[...]
    a = a_ref[pl.ds(NI * ia, NI), :]
    aa = jnp.concatenate([a, a], axis=1)
    a_turned = jnp.concatenate([aa, aa], axis=0).T[:R, :]
    bt = b.T[:R, :]
    third = None
    for i in range(NI):
        x = jnp.concatenate(split(bt * a_turned[:, i : i + 1]), axis=0)
        t_hi, t_lo = split(t_ref[i])
        part = dot(x, t_hi) + dot(x, t_lo)
        third = part if third is None else third + part
    gram_b = dot(jnp.concatenate(split(bt), axis=0), parts(b))
    gram_b = twice(gram_b[:R, :] + gram_b[R:, :])
    gram_a = a_turned[:, 0:1] * aa[0:1, :]
    for i in range(1, NI):
        gram_a = gram_a + a_turned[:, i : i + 1] * aa[i : i + 1, :]
    gram = parts(gram_a * gram_b)
    row = jnp.sum(r2_ref[pl.ds(8, NK, stride=M2), :], axis=0, keepdims=True)
    place = lax.broadcasted_iota(jnp.int32, (R, R), 0)
    mine = jnp.where(place == 2 * p, row[:, :R], jnp.where(place == 2 * p + 1, row[:, R:], 0.0))
    rows = r1_ref[pl.ds(4, NP, stride=M1), :]
    grad_b = dot_exact(jnp.concatenate([rows[:, :R], rows[:, R:]], axis=0), mine, ((1,), (0,)))
    grad_b = jnp.concatenate([grad_b[:NP, :], grad_b[NP:, :]], axis=1)
    summed = jnp.concatenate(
        [
            jnp.broadcast_to(
                jnp.sum(r2_ref[pl.ds(4 + i, NK, stride=M2), :], axis=0, keepdims=True), (NJ, W)
            )
            for i in range(NI)
        ],
        axis=0,
    )
    peer = slot(lax.broadcasted_iota(jnp.int32, (NP, W), 0))
    grad_b = grad_b - jnp.where(lax.rem(peer, NJ) == ja, summed, 0.0)
    out_ref[pl.ds(4, NP, stride=M3), :] = grad_b
    third = twice(dot(cc_ref[...], jnp.concatenate([gram, gram], axis=0)) - third.T)
    third_ref[...] = swapped(third)
    for q in range(4):
        left = third_ref[pl.ds(q, NP, stride=8), :]
        right = third_ref[pl.ds(q + 4, NP, stride=8), :]
        out_ref[pl.ds(q, NP, stride=M3), :] = join(left, right)


def final_kernel(r3_ref, gb_ref, gc_ref):
    for q in range(4):
        row = jnp.sum(r3_ref[pl.ds(q, NP, stride=M3), :], axis=0, keepdims=True)
        gc_ref[q : q + 1, :] = row[:, :R]
        gc_ref[q + 4 : q + 5, :] = row[:, R:]
    row = jnp.sum(r3_ref[pl.ds(4, NP, stride=M3), :], axis=0, keepdims=True)
    gb_ref[0:1, :] = row[:, :R]
    gb_ref[1:2, :] = row[:, R:]


def call(kernel, outs, operands, scratch=(), copies=0, in_hbm=0, kinds=None):
    kinds = kinds or [F32] * len(outs)
    scratch_shapes = [pltpu.VMEM(shape, F32) for shape in scratch]
    if copies:
        scratch_shapes.append(pltpu.SemaphoreType.DMA((copies,)))
    return pl.pallas_call(
        kernel,
        out_shape=[jax.ShapeDtypeStruct(shape, kind) for shape, kind in zip(outs, kinds)],
        in_specs=[HBM] * in_hbm + [VMEM] * (len(operands) - in_hbm),
        out_specs=[VMEM] * len(outs),
        scratch_shapes=scratch_shapes,
        compiler_params=pltpu.CompilerParams(vmem_limit_bytes=16 * 1024 * 1024),
        cost_estimate=pl.CostEstimate(flops=10**9, bytes_accessed=NP * M1 * W * 4, transcendentals=0),
    )(*[pltpu.with_memory_space_constraint(x, pltpu.HBM) for x in operands[:in_hbm]], *operands[in_hbm:])


def exchange(x, axes, rows, head):
    peers = x.shape[0] // rows
    order = list(range(peers))
    order[0], order[head] = head, 0
    x = x.reshape(peers, rows, 1, W)
    x = lax.all_to_all(x, axes, 0, 0, axis_index_groups=[order])
    return x.reshape(peers * rows, W)


def per_device(tensor, factor_a, factor_b, factor_c):
    s1 = pl.pallas_call(
        pack_kernel,
        out_shape=pltpu.VMEM((NP * M1, W), F32),
        in_specs=[HBM] * 2,
        out_specs=VMEM,
        scratch_shapes=[
            pltpu.VMEM((2, R), F32),
            pltpu.VMEM((8, R), F32),
            pltpu.SemaphoreType.DMA((2,)),
        ],
        compiler_params=pltpu.CompilerParams(vmem_limit_bytes=16 * 1024 * 1024),
        cost_estimate=pl.CostEstimate(flops=10**9, bytes_accessed=NP * M1 * W * 4, transcendentals=0),
    )(*[pltpu.with_memory_space_constraint(x, pltpu.HBM) for x in (factor_b, factor_c)])
    block = tensor
    r1 = exchange(s1, ("ia", "ja"), M1, HEAD_P)
    s2, cc = call(
        second_kernel,
        [(NK * M2, W), (ROWS, W)],
        (block, factor_a, r1),
        [(ROWS, W), (16, W), (R, W)],
        kinds=[F32, BF16],
    )
    r2 = exchange(s2, "ka", M2, HEAD_K)
    (s3,) = call(
        third_kernel,
        [(NP * M3, W)],
        (block, factor_a, cc, r1, r2),
        [(ROWS, W), (ROWS, W)],
    )
    r3 = exchange(s3, ("ia", "ja"), M3, HEAD_P)
    return tuple(call(final_kernel, [(2, R), (8, R)], (r3,)))


def solution(mesh):
    placed = (P("ia", "ja", "ka"), P(), P(("ja", "ia", "ka"), None), P(("ka", "ia", "ja"), None))
    return jax.shard_map(
        per_device,
        mesh=mesh,
        in_specs=placed,
        out_specs=(P(("ja", "ia", "ka"), None), P(("ka", "ia", "ja"), None)),
        check_vma=False,
    )
```

```python
import jax
import jax.numpy as jnp
from jax import lax
from jax.experimental import pallas as pl
from jax.experimental.pallas import tpu as pltpu
from jax.sharding import PartitionSpec as P

F32 = jnp.float32
BF16 = jnp.bfloat16
VMEM = pl.BlockSpec(memory_space=pltpu.VMEM)
HBM = pl.BlockSpec(memory_space=pltpu.HBM)

NI, NJ, NK = 4, 8, 32
NP = NI * NJ
R = 64
W = 2 * R
ROWS = 256
M1, M2, M3 = 5, 9, 5
HEAD_P, HEAD_K = 12, 26


def coords():
    return lax.axis_index("ia"), lax.axis_index("ja")


def rough(x):
    return x.astype(BF16).astype(F32)


def dot(x, y, dims=((1,), (0,))):
    return lax.dot_general(x, y, (dims, ((), ())), preferred_element_type=F32)


def dot_exact(x, y, dims):
    return lax.dot_general(
        x, y, (dims, ((), ())), precision=lax.Precision.HIGHEST, preferred_element_type=F32
    )


def left_half(x):
    return lax.broadcasted_iota(jnp.int32, x.shape, 1) < R


def join(x, y):
    return jnp.where(left_half(x), x, y)


def slot(p):
    return jnp.where(p == 0, HEAD_P, jnp.where(p == HEAD_P, 0, p))


def swapped(x):
    head = 8 * HEAD_P
    return jnp.concatenate([x[head : head + 8], x[8:head], x[:8], x[head + 8 :]], axis=0)


def turned(x):
    return pltpu.roll(x, R, 1)


def twice(x):
    return x + turned(x)


def parts(x):
    return join(x, x - rough(x)).astype(BF16)


def split(x):
    hi = rough(x)
    return x.astype(BF16), (x - hi).astype(BF16)


def fetch(source, target, sem):
    copy = pltpu.make_async_copy(source, target, sem)
    copy.start()
    return copy


def pack_kernel(b_hbm, c_hbm, out_ref, b_ref, c_ref, sems):
    copies = [fetch(b_hbm, b_ref, sems.at[0]), fetch(c_hbm, c_ref, sems.at[1])]
    for copy in copies:
        copy.wait()
    for q in range(4):
        row = jnp.concatenate([c_ref[q : q + 1, :], c_ref[q + 4 : q + 5, :]], axis=1)
        out_ref[pl.ds(q, NP, stride=M1), :] = jnp.broadcast_to(row, (NP, W))
    row = jnp.concatenate([b_ref[0:1, :], b_ref[1:2, :]], axis=1)
    out_ref[pl.ds(4, NP, stride=M1), :] = jnp.broadcast_to(row, (NP, W))


def second_kernel(t_ref, a_ref, r1_ref, out_ref, cc_ref, c_ref, sec_ref, gram_ref):
    ia, ja = coords()
    p = ia * NJ + ja
    for q in range(4):
        rows = r1_ref[pl.ds(q, NP, stride=M1), :]
        other = turned(rows)
        c_ref[pl.ds(q, NP, stride=8), :] = join(rows, other)
        c_ref[pl.ds(q + 4, NP, stride=8), :] = join(other, rows)
    c = swapped(c_ref[...])
    a = a_ref[...]
    aa = jnp.concatenate([a, a], axis=1)
    cc = parts(c)
    cc_ref[...] = cc
    gram_a = dot_exact(a, aa, ((0,), (0,)))
    gram_c = dot(cc, cc, ((0,), (0,)))
    gram_ref[...] = gram_a * twice(gram_c[:R, :] + gram_c[R:, :])
    sec_ref[...] = aa
    weights = [parts(c * sec_ref[pl.ds(NI * ia + i, 1), :]) for i in range(NI)]
    second = None
    for i in range(NI):
        t_hi, t_lo = split(t_ref[i])
        part = dot(t_hi, weights[i]) + dot(t_lo, weights[i])
        second = part if second is None else second + part
    row = join(gram_ref[pl.ds(2 * p, 1), :], gram_ref[pl.ds(2 * p + 1, 1), :])
    out_ref[pl.ds(8, NK, stride=M2), :] = jnp.broadcast_to(row, (NK, W))
    for i in range(NI):
        row = r1_ref[pl.ds(slot(i * NJ + ja) * M1 + 4, 1), :]
        out_ref[pl.ds(i, NK, stride=M2), :] = jnp.broadcast_to(row, (NK, W))
    c_ref[...] = second
    for i in range(NI):
        even = c_ref[pl.ds(i * 2 * NK, NK, stride=2), :]
        odd = c_ref[pl.ds(i * 2 * NK + 1, NK, stride=2), :]
        out_ref[pl.ds(4 + i, NK, stride=M2), :] = join(twice(even), twice(odd))
    head = HEAD_K * M2
    first, last = out_ref[4:8, :], out_ref[head + 4 : head + 8, :]
    out_ref[4:8, :] = last
    out_ref[head + 4 : head + 8, :] = first


def third_kernel(t_ref, a_ref, cc_ref, r1_ref, r2_ref, out_ref, b_ref, third_ref):
    ia, ja = coords()
    p = ia * NJ + ja
    for i in range(NI):
        rows = r2_ref[pl.ds(i, NK, stride=M2), :]
        other = turned(rows)
        b_ref[pl.ds(i * 2 * NK, NK, stride=2), :] = join(rows, other)
        b_ref[pl.ds(i * 2 * NK + 1, NK, stride=2), :] = join(other, rows)
        for ka, place in ((0, HEAD_K), (HEAD_K, 0)):
            row = r2_ref[place * M2 + i : place * M2 + i + 1, :]
            start = i * 2 * NK + 2 * ka
            b_ref[start : start + 1, :] = join(row, turned(row))
            b_ref[start + 1 : start + 2, :] = join(turned(row), row)
    b = b_ref[...]
    a = a_ref[pl.ds(NI * ia, NI), :]
    aa = jnp.concatenate([a, a], axis=1)
    a_turned = jnp.concatenate([aa, aa], axis=0).T[:R, :]
    bt = b.T[:R, :]
    third = None
    for i in range(NI):
        x = jnp.concatenate(split(bt * a_turned[:, i : i + 1]), axis=0)
        t_hi, t_lo = split(t_ref[i])
        part = dot(x, t_hi) + dot(x, t_lo)
        third = part if third is None else third + part
    gram_b = dot(jnp.concatenate(split(bt), axis=0), parts(b))
    gram_b = twice(gram_b[:R, :] + gram_b[R:, :])
    gram_a = a_turned[:, 0:1] * aa[0:1, :]
    for i in range(1, NI):
        gram_a = gram_a + a_turned[:, i : i + 1] * aa[i : i + 1, :]
    gram = parts(gram_a * gram_b)
    row = jnp.sum(r2_ref[pl.ds(8, NK, stride=M2), :], axis=0, keepdims=True)
    place = lax.broadcasted_iota(jnp.int32, (R, R), 0)
    mine = jnp.where(place == 2 * p, row[:, :R], jnp.where(place == 2 * p + 1, row[:, R:], 0.0))
    rows = r1_ref[pl.ds(4, NP, stride=M1), :]
    grad_b = dot_exact(jnp.concatenate([rows[:, :R], rows[:, R:]], axis=0), mine, ((1,), (0,)))
    grad_b = jnp.concatenate([grad_b[:NP, :], grad_b[NP:, :]], axis=1)
    peer = slot(lax.broadcasted_iota(jnp.int32, (NP, W), 0))
    for i in range(NI):
        row = jnp.sum(r2_ref[pl.ds(4 + i, NK, stride=M2), :], axis=0, keepdims=True)
        grad_b = grad_b - jnp.where(peer == i * NJ + ja, row, 0.0)
    out_ref[pl.ds(4, NP, stride=M3), :] = grad_b
    third = twice(dot(cc_ref[...], jnp.concatenate([gram, gram], axis=0)) - third.T)
    third_ref[...] = swapped(third)
    for q in range(4):
        left = third_ref[pl.ds(q, NP, stride=8), :]
        right = third_ref[pl.ds(q + 4, NP, stride=8), :]
        out_ref[pl.ds(q, NP, stride=M3), :] = join(left, right)


def final_kernel(r3_ref, gb_ref, gc_ref):
    for q in range(4):
        row = jnp.sum(r3_ref[pl.ds(q, NP, stride=M3), :], axis=0, keepdims=True)
        gc_ref[q : q + 1, :] = row[:, :R]
        gc_ref[q + 4 : q + 5, :] = row[:, R:]
    row = jnp.sum(r3_ref[pl.ds(4, NP, stride=M3), :], axis=0, keepdims=True)
    gb_ref[0:1, :] = row[:, :R]
    gb_ref[1:2, :] = row[:, R:]


def call(kernel, outs, operands, scratch=(), copies=0, in_hbm=0, kinds=None):
    kinds = kinds or [F32] * len(outs)
    scratch_shapes = [pltpu.VMEM(shape, F32) for shape in scratch]
    if copies:
        scratch_shapes.append(pltpu.SemaphoreType.DMA((copies,)))
    return pl.pallas_call(
        kernel,
        out_shape=[jax.ShapeDtypeStruct(shape, kind) for shape, kind in zip(outs, kinds)],
        in_specs=[HBM] * in_hbm + [VMEM] * (len(operands) - in_hbm),
        out_specs=[VMEM] * len(outs),
        scratch_shapes=scratch_shapes,
        compiler_params=pltpu.CompilerParams(vmem_limit_bytes=16 * 1024 * 1024),
        cost_estimate=pl.CostEstimate(flops=10**9, bytes_accessed=NP * M1 * W * 4, transcendentals=0),
    )(*[pltpu.with_memory_space_constraint(x, pltpu.HBM) for x in operands[:in_hbm]], *operands[in_hbm:])


def exchange(x, axes, rows, head):
    peers = x.shape[0] // rows
    order = list(range(peers))
    order[0], order[head] = head, 0
    x = x.reshape(peers, rows, 1, W)
    x = lax.all_to_all(x, axes, 0, 0, axis_index_groups=[order])
    return x.reshape(peers * rows, W)


def per_device(tensor, factor_a, factor_b, factor_c):
    s1 = pl.pallas_call(
        pack_kernel,
        out_shape=pltpu.VMEM((NP * M1, W), F32),
        in_specs=[HBM] * 2,
        out_specs=VMEM,
        scratch_shapes=[
            pltpu.VMEM((2, R), F32),
            pltpu.VMEM((8, R), F32),
            pltpu.SemaphoreType.DMA((2,)),
        ],
        compiler_params=pltpu.CompilerParams(vmem_limit_bytes=16 * 1024 * 1024),
        cost_estimate=pl.CostEstimate(flops=10**9, bytes_accessed=NP * M1 * W * 4, transcendentals=0),
    )(*[pltpu.with_memory_space_constraint(x, pltpu.HBM) for x in (factor_b, factor_c)])
    block = tensor
    r1 = exchange(s1, ("ia", "ja"), M1, HEAD_P)
    s2, cc = call(
        second_kernel,
        [(NK * M2, W), (ROWS, W)],
        (block, factor_a, r1),
        [(ROWS, W), (16, W), (R, W)],
        kinds=[F32, BF16],
    )
    r2 = exchange(s2, "ka", M2, HEAD_K)
    (s3,) = call(
        third_kernel,
        [(NP * M3, W)],
        (block, factor_a, cc, r1, r2),
        [(ROWS, W), (ROWS, W)],
    )
    r3 = exchange(s3, ("ia", "ja"), M3, HEAD_P)
    return tuple(call(final_kernel, [(2, R), (8, R)], (r3,)))


def solution(mesh):
    placed = (P("ia", "ja", "ka"), P(), P(("ja", "ia", "ka"), None), P(("ka", "ia", "ja"), None))
    return jax.shard_map(
        per_device,
        mesh=mesh,
        in_specs=placed,
        out_specs=(P(("ja", "ia", "ka"), None), P(("ka", "ia", "ja"), None)),
        check_vma=False,
    )
```

```python
import jax
import jax.numpy as jnp
from jax import lax
from jax.experimental import pallas as pl
from jax.experimental.pallas import tpu as pltpu
from jax.sharding import PartitionSpec as P

F32 = jnp.float32
BF16 = jnp.bfloat16
VMEM = pl.BlockSpec(memory_space=pltpu.VMEM)
HBM = pl.BlockSpec(memory_space=pltpu.HBM)

NI, NJ, NK = 4, 8, 32
NP = NI * NJ
R = 64
W = 2 * R
ROWS = 256
M1, M2, M3 = 5, 9, 5
HEAD_P, HEAD_K = 13, 26


def coords():
    return lax.axis_index("ia"), lax.axis_index("ja")


def rough(x):
    return x.astype(BF16).astype(F32)


def dot(x, y, dims=((1,), (0,))):
    return lax.dot_general(x, y, (dims, ((), ())), preferred_element_type=F32)


def dot_exact(x, y, dims):
    return lax.dot_general(
        x, y, (dims, ((), ())), precision=lax.Precision.HIGHEST, preferred_element_type=F32
    )


def left_half(x):
    return lax.broadcasted_iota(jnp.int32, x.shape, 1) < R


def join(x, y):
    return jnp.where(left_half(x), x, y)


def slot(p):
    return jnp.where(p == 0, HEAD_P, jnp.where(p == HEAD_P, 0, p))


def swapped(x):
    head = 8 * HEAD_P
    return jnp.concatenate([x[head : head + 8], x[8:head], x[:8], x[head + 8 :]], axis=0)


def turned(x):
    return pltpu.roll(x, R, 1)


def twice(x):
    return x + turned(x)


def parts(x):
    return join(x, x - rough(x)).astype(BF16)


def split(x):
    hi = rough(x)
    return x.astype(BF16), (x - hi).astype(BF16)


def fetch(source, target, sem):
    copy = pltpu.make_async_copy(source, target, sem)
    copy.start()
    return copy


def pack_kernel(b_hbm, c_hbm, out_ref, b_ref, c_ref, sems):
    copies = [fetch(b_hbm, b_ref, sems.at[0]), fetch(c_hbm, c_ref, sems.at[1])]
    for copy in copies:
        copy.wait()
    for q in range(4):
        row = jnp.concatenate([c_ref[q : q + 1, :], c_ref[q + 4 : q + 5, :]], axis=1)
        out_ref[pl.ds(q, NP, stride=M1), :] = jnp.broadcast_to(row, (NP, W))
    row = jnp.concatenate([b_ref[0:1, :], b_ref[1:2, :]], axis=1)
    out_ref[pl.ds(4, NP, stride=M1), :] = jnp.broadcast_to(row, (NP, W))


def second_kernel(t_ref, a_ref, r1_ref, out_ref, cc_ref, c_ref, sec_ref, gram_ref):
    ia, ja = coords()
    p = ia * NJ + ja
    for q in range(4):
        rows = r1_ref[pl.ds(q, NP, stride=M1), :]
        other = turned(rows)
        c_ref[pl.ds(q, NP, stride=8), :] = join(rows, other)
        c_ref[pl.ds(q + 4, NP, stride=8), :] = join(other, rows)
    c = swapped(c_ref[...])
    a = a_ref[...]
    aa = jnp.concatenate([a, a], axis=1)
    cc = parts(c)
    cc_ref[...] = cc
    gram_a = dot_exact(a, aa, ((0,), (0,)))
    gram_c = dot(cc, cc, ((0,), (0,)))
    gram_ref[...] = gram_a * twice(gram_c[:R, :] + gram_c[R:, :])
    sec_ref[...] = aa
    weights = [parts(c * sec_ref[pl.ds(NI * ia + i, 1), :]) for i in range(NI)]
    second = None
    for i in range(NI):
        t_hi, t_lo = split(t_ref[i])
        part = dot(t_hi, weights[i]) + dot(t_lo, weights[i])
        second = part if second is None else second + part
    row = join(gram_ref[pl.ds(2 * p, 1), :], gram_ref[pl.ds(2 * p + 1, 1), :])
    out_ref[pl.ds(8, NK, stride=M2), :] = jnp.broadcast_to(row, (NK, W))
    for i in range(NI):
        row = r1_ref[pl.ds(slot(i * NJ + ja) * M1 + 4, 1), :]
        out_ref[pl.ds(i, NK, stride=M2), :] = jnp.broadcast_to(row, (NK, W))
    c_ref[...] = second
    for i in range(NI):
        even = c_ref[pl.ds(i * 2 * NK, NK, stride=2), :]
        odd = c_ref[pl.ds(i * 2 * NK + 1, NK, stride=2), :]
        out_ref[pl.ds(4 + i, NK, stride=M2), :] = join(twice(even), twice(odd))
    head = HEAD_K * M2
    first, last = out_ref[4:8, :], out_ref[head + 4 : head + 8, :]
    out_ref[4:8, :] = last
    out_ref[head + 4 : head + 8, :] = first


def third_kernel(t_ref, a_ref, cc_ref, r1_ref, r2_ref, out_ref, b_ref, third_ref):
    ia, ja = coords()
    p = ia * NJ + ja
    for i in range(NI):
        rows = r2_ref[pl.ds(i, NK, stride=M2), :]
        other = turned(rows)
        b_ref[pl.ds(i * 2 * NK, NK, stride=2), :] = join(rows, other)
        b_ref[pl.ds(i * 2 * NK + 1, NK, stride=2), :] = join(other, rows)
        for ka, place in ((0, HEAD_K), (HEAD_K, 0)):
            row = r2_ref[place * M2 + i : place * M2 + i + 1, :]
            start = i * 2 * NK + 2 * ka
            b_ref[start : start + 1, :] = join(row, turned(row))
            b_ref[start + 1 : start + 2, :] = join(turned(row), row)
    b = b_ref[...]
    a = a_ref[pl.ds(NI * ia, NI), :]
    aa = jnp.concatenate([a, a], axis=1)
    a_turned = jnp.concatenate([aa, aa], axis=0).T[:R, :]
    bt = b.T[:R, :]
    third = None
    for i in range(NI):
        x = jnp.concatenate(split(bt * a_turned[:, i : i + 1]), axis=0)
        t_hi, t_lo = split(t_ref[i])
        part = dot(x, t_hi) + dot(x, t_lo)
        third = part if third is None else third + part
    gram_b = dot(jnp.concatenate(split(bt), axis=0), parts(b))
    gram_b = twice(gram_b[:R, :] + gram_b[R:, :])
    gram_a = a_turned[:, 0:1] * aa[0:1, :]
    for i in range(1, NI):
        gram_a = gram_a + a_turned[:, i : i + 1] * aa[i : i + 1, :]
    gram = parts(gram_a * gram_b)
    row = jnp.sum(r2_ref[pl.ds(8, NK, stride=M2), :], axis=0, keepdims=True)
    place = lax.broadcasted_iota(jnp.int32, (R, R), 0)
    mine = jnp.where(place == 2 * p, row[:, :R], jnp.where(place == 2 * p + 1, row[:, R:], 0.0))
    rows = r1_ref[pl.ds(4, NP, stride=M1), :]
    grad_b = dot_exact(jnp.concatenate([rows[:, :R], rows[:, R:]], axis=0), mine, ((1,), (0,)))
    grad_b = jnp.concatenate([grad_b[:NP, :], grad_b[NP:, :]], axis=1)
    peer = slot(lax.broadcasted_iota(jnp.int32, (NP, W), 0))
    for i in range(NI):
        row = jnp.sum(r2_ref[pl.ds(4 + i, NK, stride=M2), :], axis=0, keepdims=True)
        grad_b = grad_b - jnp.where(peer == i * NJ + ja, row, 0.0)
    out_ref[pl.ds(4, NP, stride=M3), :] = grad_b
    third = twice(dot(cc_ref[...], jnp.concatenate([gram, gram], axis=0)) - third.T)
    third_ref[...] = swapped(third)
    for q in range(4):
        left = third_ref[pl.ds(q, NP, stride=8), :]
        right = third_ref[pl.ds(q + 4, NP, stride=8), :]
        out_ref[pl.ds(q, NP, stride=M3), :] = join(left, right)


def final_kernel(r3_ref, gb_ref, gc_ref):
    for q in range(4):
        row = jnp.sum(r3_ref[pl.ds(q, NP, stride=M3), :], axis=0, keepdims=True)
        gc_ref[q : q + 1, :] = row[:, :R]
        gc_ref[q + 4 : q + 5, :] = row[:, R:]
    row = jnp.sum(r3_ref[pl.ds(4, NP, stride=M3), :], axis=0, keepdims=True)
    gb_ref[0:1, :] = row[:, :R]
    gb_ref[1:2, :] = row[:, R:]


def call(kernel, outs, operands, scratch=(), copies=0, in_hbm=0, kinds=None):
    kinds = kinds or [F32] * len(outs)
    scratch_shapes = [pltpu.VMEM(shape, F32) for shape in scratch]
    if copies:
        scratch_shapes.append(pltpu.SemaphoreType.DMA((copies,)))
    return pl.pallas_call(
        kernel,
        out_shape=[jax.ShapeDtypeStruct(shape, kind) for shape, kind in zip(outs, kinds)],
        in_specs=[HBM] * in_hbm + [VMEM] * (len(operands) - in_hbm),
        out_specs=[VMEM] * len(outs),
        scratch_shapes=scratch_shapes,
        compiler_params=pltpu.CompilerParams(vmem_limit_bytes=16 * 1024 * 1024),
        cost_estimate=pl.CostEstimate(flops=10**9, bytes_accessed=NP * M1 * W * 4, transcendentals=0),
    )(*[pltpu.with_memory_space_constraint(x, pltpu.HBM) for x in operands[:in_hbm]], *operands[in_hbm:])


def exchange(x, axes, rows, head):
    peers = x.shape[0] // rows
    order = list(range(peers))
    order[0], order[head] = head, 0
    x = x.reshape(peers, rows, 1, W)
    x = lax.all_to_all(x, axes, 0, 0, axis_index_groups=[order])
    return x.reshape(peers * rows, W)


def per_device(tensor, factor_a, factor_b, factor_c):
    s1 = pl.pallas_call(
        pack_kernel,
        out_shape=pltpu.VMEM((NP * M1, W), F32),
        in_specs=[HBM] * 2,
        out_specs=VMEM,
        scratch_shapes=[
            pltpu.VMEM((2, R), F32),
            pltpu.VMEM((8, R), F32),
            pltpu.SemaphoreType.DMA((2,)),
        ],
        compiler_params=pltpu.CompilerParams(vmem_limit_bytes=16 * 1024 * 1024),
        cost_estimate=pl.CostEstimate(flops=10**9, bytes_accessed=NP * M1 * W * 4, transcendentals=0),
    )(*[pltpu.with_memory_space_constraint(x, pltpu.HBM) for x in (factor_b, factor_c)])
    block = tensor
    r1 = exchange(s1, ("ia", "ja"), M1, HEAD_P)
    s2, cc = call(
        second_kernel,
        [(NK * M2, W), (ROWS, W)],
        (block, factor_a, r1),
        [(ROWS, W), (16, W), (R, W)],
        kinds=[F32, BF16],
    )
    r2 = exchange(s2, "ka", M2, HEAD_K)
    (s3,) = call(
        third_kernel,
        [(NP * M3, W)],
        (block, factor_a, cc, r1, r2),
        [(ROWS, W), (ROWS, W)],
    )
    r3 = exchange(s3, ("ia", "ja"), M3, HEAD_P)
    return tuple(call(final_kernel, [(2, R), (8, R)], (r3,)))


def solution(mesh):
    placed = (P("ia", "ja", "ka"), P(), P(("ja", "ia", "ka"), None), P(("ka", "ia", "ja"), None))
    return jax.shard_map(
        per_device,
        mesh=mesh,
        in_specs=placed,
        out_specs=(P(("ja", "ia", "ka"), None), P(("ka", "ia", "ja"), None)),
        check_vma=False,
    )
```

```python
import jax
import jax.numpy as jnp
from jax import lax
from jax.experimental import pallas as pl
from jax.experimental.pallas import tpu as pltpu
from jax.sharding import PartitionSpec as P

F32 = jnp.float32
BF16 = jnp.bfloat16
VMEM = pl.BlockSpec(memory_space=pltpu.VMEM)
HBM = pl.BlockSpec(memory_space=pltpu.HBM)

NI, NJ, NK = 4, 8, 32
NP = NI * NJ
R = 64
W = 2 * R
ROWS = 256
M1, M2, M3 = 5, 9, 5
HEAD_P, HEAD_K = 12, 22


def coords():
    return lax.axis_index("ia"), lax.axis_index("ja")


def rough(x):
    return x.astype(BF16).astype(F32)


def dot(x, y, dims=((1,), (0,))):
    return lax.dot_general(x, y, (dims, ((), ())), preferred_element_type=F32)


def dot_exact(x, y, dims):
    return lax.dot_general(
        x, y, (dims, ((), ())), precision=lax.Precision.HIGHEST, preferred_element_type=F32
    )


def left_half(x):
    return lax.broadcasted_iota(jnp.int32, x.shape, 1) < R


def join(x, y):
    return jnp.where(left_half(x), x, y)


def slot(p):
    return jnp.where(p == 0, HEAD_P, jnp.where(p == HEAD_P, 0, p))


def swapped(x):
    head = 8 * HEAD_P
    return jnp.concatenate([x[head : head + 8], x[8:head], x[:8], x[head + 8 :]], axis=0)


def turned(x):
    return pltpu.roll(x, R, 1)


def twice(x):
    return x + turned(x)


def parts(x):
    return join(x, x - rough(x)).astype(BF16)


def split(x):
    hi = rough(x)
    return x.astype(BF16), (x - hi).astype(BF16)


def fetch(source, target, sem):
    copy = pltpu.make_async_copy(source, target, sem)
    copy.start()
    return copy


def pack_kernel(b_hbm, c_hbm, out_ref, b_ref, c_ref, sems):
    copies = [fetch(b_hbm, b_ref, sems.at[0]), fetch(c_hbm, c_ref, sems.at[1])]
    for copy in copies:
        copy.wait()
    for q in range(4):
        row = jnp.concatenate([c_ref[q : q + 1, :], c_ref[q + 4 : q + 5, :]], axis=1)
        out_ref[pl.ds(q, NP, stride=M1), :] = jnp.broadcast_to(row, (NP, W))
    row = jnp.concatenate([b_ref[0:1, :], b_ref[1:2, :]], axis=1)
    out_ref[pl.ds(4, NP, stride=M1), :] = jnp.broadcast_to(row, (NP, W))


def second_kernel(t_ref, a_ref, r1_ref, out_ref, cc_ref, c_ref, sec_ref, gram_ref):
    ia, ja = coords()
    p = ia * NJ + ja
    for q in range(4):
        rows = r1_ref[pl.ds(q, NP, stride=M1), :]
        other = turned(rows)
        c_ref[pl.ds(q, NP, stride=8), :] = join(rows, other)
        c_ref[pl.ds(q + 4, NP, stride=8), :] = join(other, rows)
    c = swapped(c_ref[...])
    a = a_ref[...]
    aa = jnp.concatenate([a, a], axis=1)
    cc = parts(c)
    cc_ref[...] = cc
    gram_a = dot_exact(a, aa, ((0,), (0,)))
    gram_c = dot(cc, cc, ((0,), (0,)))
    gram_ref[...] = gram_a * twice(gram_c[:R, :] + gram_c[R:, :])
    sec_ref[...] = aa
    weights = [parts(c * sec_ref[pl.ds(NI * ia + i, 1), :]) for i in range(NI)]
    second = None
    for i in range(NI):
        t_hi, t_lo = split(t_ref[i])
        part = dot(t_hi, weights[i]) + dot(t_lo, weights[i])
        second = part if second is None else second + part
    row = join(gram_ref[pl.ds(2 * p, 1), :], gram_ref[pl.ds(2 * p + 1, 1), :])
    out_ref[pl.ds(8, NK, stride=M2), :] = jnp.broadcast_to(row, (NK, W))
    for i in range(NI):
        row = r1_ref[pl.ds(slot(i * NJ + ja) * M1 + 4, 1), :]
        out_ref[pl.ds(i, NK, stride=M2), :] = jnp.broadcast_to(row, (NK, W))
    c_ref[...] = second
    for i in range(NI):
        even = c_ref[pl.ds(i * 2 * NK, NK, stride=2), :]
        odd = c_ref[pl.ds(i * 2 * NK + 1, NK, stride=2), :]
        out_ref[pl.ds(4 + i, NK, stride=M2), :] = join(twice(even), twice(odd))
    head = HEAD_K * M2
    first, last = out_ref[4:8, :], out_ref[head + 4 : head + 8, :]
    out_ref[4:8, :] = last
    out_ref[head + 4 : head + 8, :] = first


def third_kernel(t_ref, a_ref, cc_ref, r1_ref, r2_ref, out_ref, b_ref, third_ref):
    ia, ja = coords()
    p = ia * NJ + ja
    for i in range(NI):
        rows = r2_ref[pl.ds(i, NK, stride=M2), :]
        other = turned(rows)
        b_ref[pl.ds(i * 2 * NK, NK, stride=2), :] = join(rows, other)
        b_ref[pl.ds(i * 2 * NK + 1, NK, stride=2), :] = join(other, rows)
        for ka, place in ((0, HEAD_K), (HEAD_K, 0)):
            row = r2_ref[place * M2 + i : place * M2 + i + 1, :]
            start = i * 2 * NK + 2 * ka
            b_ref[start : start + 1, :] = join(row, turned(row))
            b_ref[start + 1 : start + 2, :] = join(turned(row), row)
    b = b_ref[...]
    a = a_ref[pl.ds(NI * ia, NI), :]
    aa = jnp.concatenate([a, a], axis=1)
    a_turned = jnp.concatenate([aa, aa], axis=0).T[:R, :]
    bt = b.T[:R, :]
    third = None
    for i in range(NI):
        x = jnp.concatenate(split(bt * a_turned[:, i : i + 1]), axis=0)
        t_hi, t_lo = split(t_ref[i])
        part = dot(x, t_hi) + dot(x, t_lo)
        third = part if third is None else third + part
    gram_b = dot(jnp.concatenate(split(bt), axis=0), parts(b))
    gram_b = twice(gram_b[:R, :] + gram_b[R:, :])
    gram_a = a_turned[:, 0:1] * aa[0:1, :]
    for i in range(1, NI):
        gram_a = gram_a + a_turned[:, i : i + 1] * aa[i : i + 1, :]
    gram = parts(gram_a * gram_b)
    row = jnp.sum(r2_ref[pl.ds(8, NK, stride=M2), :], axis=0, keepdims=True)
    place = lax.broadcasted_iota(jnp.int32, (R, R), 0)
    mine = jnp.where(place == 2 * p, row[:, :R], jnp.where(place == 2 * p + 1, row[:, R:], 0.0))
    rows = r1_ref[pl.ds(4, NP, stride=M1), :]
    grad_b = dot_exact(jnp.concatenate([rows[:, :R], rows[:, R:]], axis=0), mine, ((1,), (0,)))
    grad_b = jnp.concatenate([grad_b[:NP, :], grad_b[NP:, :]], axis=1)
    peer = slot(lax.broadcasted_iota(jnp.int32, (NP, W), 0))
    for i in range(NI):
        row = jnp.sum(r2_ref[pl.ds(4 + i, NK, stride=M2), :], axis=0, keepdims=True)
        grad_b = grad_b - jnp.where(peer == i * NJ + ja, row, 0.0)
    out_ref[pl.ds(4, NP, stride=M3), :] = grad_b
    third = twice(dot(cc_ref[...], jnp.concatenate([gram, gram], axis=0)) - third.T)
    third_ref[...] = swapped(third)
    for q in range(4):
        left = third_ref[pl.ds(q, NP, stride=8), :]
        right = third_ref[pl.ds(q + 4, NP, stride=8), :]
        out_ref[pl.ds(q, NP, stride=M3), :] = join(left, right)


def final_kernel(r3_ref, gb_ref, gc_ref):
    for q in range(4):
        row = jnp.sum(r3_ref[pl.ds(q, NP, stride=M3), :], axis=0, keepdims=True)
        gc_ref[q : q + 1, :] = row[:, :R]
        gc_ref[q + 4 : q + 5, :] = row[:, R:]
    row = jnp.sum(r3_ref[pl.ds(4, NP, stride=M3), :], axis=0, keepdims=True)
    gb_ref[0:1, :] = row[:, :R]
    gb_ref[1:2, :] = row[:, R:]


def call(kernel, outs, operands, scratch=(), copies=0, in_hbm=0, kinds=None):
    kinds = kinds or [F32] * len(outs)
    scratch_shapes = [pltpu.VMEM(shape, F32) for shape in scratch]
    if copies:
        scratch_shapes.append(pltpu.SemaphoreType.DMA((copies,)))
    return pl.pallas_call(
        kernel,
        out_shape=[jax.ShapeDtypeStruct(shape, kind) for shape, kind in zip(outs, kinds)],
        in_specs=[HBM] * in_hbm + [VMEM] * (len(operands) - in_hbm),
        out_specs=[VMEM] * len(outs),
        scratch_shapes=scratch_shapes,
        compiler_params=pltpu.CompilerParams(vmem_limit_bytes=16 * 1024 * 1024),
        cost_estimate=pl.CostEstimate(flops=10**9, bytes_accessed=NP * M1 * W * 4, transcendentals=0),
    )(*[pltpu.with_memory_space_constraint(x, pltpu.HBM) for x in operands[:in_hbm]], *operands[in_hbm:])


def exchange(x, axes, rows, head):
    peers = x.shape[0] // rows
    order = list(range(peers))
    order[0], order[head] = head, 0
    x = x.reshape(peers, rows, 1, W)
    x = lax.all_to_all(x, axes, 0, 0, axis_index_groups=[order])
    return x.reshape(peers * rows, W)


def per_device(tensor, factor_a, factor_b, factor_c):
    s1 = pl.pallas_call(
        pack_kernel,
        out_shape=pltpu.VMEM((NP * M1, W), F32),
        in_specs=[HBM] * 2,
        out_specs=VMEM,
        scratch_shapes=[
            pltpu.VMEM((2, R), F32),
            pltpu.VMEM((8, R), F32),
            pltpu.SemaphoreType.DMA((2,)),
        ],
        compiler_params=pltpu.CompilerParams(vmem_limit_bytes=16 * 1024 * 1024),
        cost_estimate=pl.CostEstimate(flops=10**9, bytes_accessed=NP * M1 * W * 4, transcendentals=0),
    )(*[pltpu.with_memory_space_constraint(x, pltpu.HBM) for x in (factor_b, factor_c)])
    block = tensor
    r1 = exchange(s1, ("ia", "ja"), M1, HEAD_P)
    s2, cc = call(
        second_kernel,
        [(NK * M2, W), (ROWS, W)],
        (block, factor_a, r1),
        [(ROWS, W), (16, W), (R, W)],
        kinds=[F32, BF16],
    )
    r2 = exchange(s2, "ka", M2, HEAD_K)
    (s3,) = call(
        third_kernel,
        [(NP * M3, W)],
        (block, factor_a, cc, r1, r2),
        [(ROWS, W), (ROWS, W)],
    )
    r3 = exchange(s3, ("ia", "ja"), M3, HEAD_P)
    return tuple(call(final_kernel, [(2, R), (8, R)], (r3,)))


def solution(mesh):
    placed = (P("ia", "ja", "ka"), P(), P(("ja", "ia", "ka"), None), P(("ka", "ia", "ja"), None))
    return jax.shard_map(
        per_device,
        mesh=mesh,
        in_specs=placed,
        out_specs=(P(("ja", "ia", "ka"), None), P(("ka", "ia", "ja"), None)),
        check_vma=False,
    )
```

```python
import jax
import jax.numpy as jnp
from jax import lax
from jax.experimental import pallas as pl
from jax.experimental.pallas import tpu as pltpu
from jax.sharding import PartitionSpec as P

F32 = jnp.float32
BF16 = jnp.bfloat16
VMEM = pl.BlockSpec(memory_space=pltpu.VMEM)
HBM = pl.BlockSpec(memory_space=pltpu.HBM)

NI, NJ, NK = 4, 8, 32
NP = NI * NJ
R = 64
W = 2 * R
ROWS = 256
M1, M2, M3 = 5, 9, 5
HEAD_P, HEAD_K = 12, 26


def coords():
    return lax.axis_index("ia"), lax.axis_index("ja")


def rough(x):
    return x.astype(BF16).astype(F32)


def dot(x, y, dims=((1,), (0,))):
    return lax.dot_general(x, y, (dims, ((), ())), preferred_element_type=F32)


def dot_exact(x, y, dims):
    return lax.dot_general(
        x, y, (dims, ((), ())), precision=lax.Precision.HIGHEST, preferred_element_type=F32
    )


def left_half(x):
    return lax.broadcasted_iota(jnp.int32, x.shape, 1) < R


def join(x, y):
    return jnp.where(left_half(x), x, y)


def slot(p):
    return jnp.where(p == 0, HEAD_P, jnp.where(p == HEAD_P, 0, p))


def swapped(x):
    head = 8 * HEAD_P
    return jnp.concatenate([x[head : head + 8], x[8:head], x[:8], x[head + 8 :]], axis=0)


def turned(x):
    return pltpu.roll(x, R, 1)


def twice(x):
    return x + turned(x)


def parts(x):
    return join(x, x - rough(x)).astype(BF16)


def split(x):
    hi = rough(x)
    return x.astype(BF16), (x - hi).astype(BF16)


def fetch(source, target, sem):
    copy = pltpu.make_async_copy(source, target, sem)
    copy.start()
    return copy


def pack_kernel(b_hbm, c_hbm, out_ref, b_ref, c_ref, sems):
    copies = [fetch(b_hbm, b_ref, sems.at[0]), fetch(c_hbm, c_ref, sems.at[1])]
    for copy in copies:
        copy.wait()
    for q in range(4):
        row = jnp.concatenate([c_ref[q : q + 1, :], c_ref[q + 4 : q + 5, :]], axis=1)
        out_ref[pl.ds(q, NP, stride=M1), :] = jnp.broadcast_to(row, (NP, W))
    row = jnp.concatenate([b_ref[0:1, :], b_ref[1:2, :]], axis=1)
    out_ref[pl.ds(4, NP, stride=M1), :] = jnp.broadcast_to(row, (NP, W))


def second_kernel(t_ref, a_ref, r1_ref, out_ref, cc_ref, c_ref, sec_ref, gram_ref):
    ia, ja = coords()
    p = ia * NJ + ja
    for q in range(4):
        rows = r1_ref[pl.ds(q, NP, stride=M1), :]
        other = turned(rows)
        c_ref[pl.ds(q, NP, stride=8), :] = join(rows, other)
        c_ref[pl.ds(q + 4, NP, stride=8), :] = join(other, rows)
    c = swapped(c_ref[...])
    a = a_ref[...]
    aa = jnp.concatenate([a, a], axis=1)
    cc = parts(c)
    cc_ref[...] = cc
    gram_a = dot_exact(a, aa, ((0,), (0,)))
    gram_c = dot(cc, cc, ((0,), (0,)))
    gram_ref[...] = gram_a * twice(gram_c[:R, :] + gram_c[R:, :])
    sec_ref[...] = aa
    weights = [parts(c * sec_ref[pl.ds(NI * ia + i, 1), :]) for i in range(NI)]
    second = None
    for i in range(NI):
        t_hi, t_lo = split(t_ref[i])
        part = dot(t_hi, weights[i]) + dot(t_lo, weights[i])
        second = part if second is None else second + part
    row = join(gram_ref[pl.ds(2 * p, 1), :], gram_ref[pl.ds(2 * p + 1, 1), :])
    out_ref[pl.ds(8, NK, stride=M2), :] = jnp.broadcast_to(row, (NK, W))
    for i in range(NI):
        row = r1_ref[pl.ds(slot(i * NJ + ja) * M1 + 4, 1), :]
        out_ref[pl.ds(i, NK, stride=M2), :] = jnp.broadcast_to(row, (NK, W))
    c_ref[...] = second
    for i in range(NI):
        even = c_ref[pl.ds(i * 2 * NK, NK, stride=2), :]
        odd = c_ref[pl.ds(i * 2 * NK + 1, NK, stride=2), :]
        out_ref[pl.ds(4 + i, NK, stride=M2), :] = join(twice(even), twice(odd))
    head = HEAD_K * M2
    first, last = out_ref[4:8, :], out_ref[head + 4 : head + 8, :]
    out_ref[4:8, :] = last
    out_ref[head + 4 : head + 8, :] = first


def third_kernel(t_ref, a_ref, cc_ref, r1_ref, r2_ref, out_ref, b_ref, third_ref):
    ia, ja = coords()
    p = ia * NJ + ja
    for i in range(NI):
        rows = r2_ref[pl.ds(i, NK, stride=M2), :]
        other = turned(rows)
        b_ref[pl.ds(i * 2 * NK, NK, stride=2), :] = join(rows, other)
        b_ref[pl.ds(i * 2 * NK + 1, NK, stride=2), :] = join(other, rows)
        for ka, place in ((0, HEAD_K), (HEAD_K, 0)):
            row = r2_ref[place * M2 + i : place * M2 + i + 1, :]
            start = i * 2 * NK + 2 * ka
            b_ref[start : start + 1, :] = join(row, turned(row))
            b_ref[start + 1 : start + 2, :] = join(turned(row), row)
    b = b_ref[...]
    a = a_ref[pl.ds(NI * ia, NI), :]
    aa = jnp.concatenate([a, a], axis=1)
    a_turned = jnp.concatenate([aa, aa], axis=0).T[:R, :]
    bt = b.T[:R, :]
    third = None
    for i in range(NI):
        x = jnp.concatenate(split(bt * a_turned[:, i : i + 1]), axis=0)
        t_hi, t_lo = split(t_ref[i])
        part = dot(x, t_hi) + dot(x, t_lo)
        third = part if third is None else third + part
    gram_b = dot(parts(b), parts(b), ((0,), (0,)))
    gram_b = twice(gram_b[:R, :] + gram_b[R:, :])
    gram_a = a_turned[:, 0:1] * aa[0:1, :]
    for i in range(1, NI):
        gram_a = gram_a + a_turned[:, i : i + 1] * aa[i : i + 1, :]
    gram = parts(gram_a * gram_b)
    row = jnp.sum(r2_ref[pl.ds(8, NK, stride=M2), :], axis=0, keepdims=True)
    place = lax.broadcasted_iota(jnp.int32, (R, R), 0)
    mine = jnp.where(place == 2 * p, row[:, :R], jnp.where(place == 2 * p + 1, row[:, R:], 0.0))
    rows = r1_ref[pl.ds(4, NP, stride=M1), :]
    grad_b = dot_exact(jnp.concatenate([rows[:, :R], rows[:, R:]], axis=0), mine, ((1,), (0,)))
    grad_b = jnp.concatenate([grad_b[:NP, :], grad_b[NP:, :]], axis=1)
    peer = slot(lax.broadcasted_iota(jnp.int32, (NP, W), 0))
    for i in range(NI):
        row = jnp.sum(r2_ref[pl.ds(4 + i, NK, stride=M2), :], axis=0, keepdims=True)
        grad_b = grad_b - jnp.where(peer == i * NJ + ja, row, 0.0)
    out_ref[pl.ds(4, NP, stride=M3), :] = grad_b
    third = twice(dot(cc_ref[...], jnp.concatenate([gram, gram], axis=0)) - third.T)
    third_ref[...] = swapped(third)
    for q in range(4):
        left = third_ref[pl.ds(q, NP, stride=8), :]
        right = third_ref[pl.ds(q + 4, NP, stride=8), :]
        out_ref[pl.ds(q, NP, stride=M3), :] = join(left, right)


def final_kernel(r3_ref, gb_ref, gc_ref):
    for q in range(4):
        row = jnp.sum(r3_ref[pl.ds(q, NP, stride=M3), :], axis=0, keepdims=True)
        gc_ref[q : q + 1, :] = row[:, :R]
        gc_ref[q + 4 : q + 5, :] = row[:, R:]
    row = jnp.sum(r3_ref[pl.ds(4, NP, stride=M3), :], axis=0, keepdims=True)
    gb_ref[0:1, :] = row[:, :R]
    gb_ref[1:2, :] = row[:, R:]


def call(kernel, outs, operands, scratch=(), copies=0, in_hbm=0, kinds=None):
    kinds = kinds or [F32] * len(outs)
    scratch_shapes = [pltpu.VMEM(shape, F32) for shape in scratch]
    if copies:
        scratch_shapes.append(pltpu.SemaphoreType.DMA((copies,)))
    return pl.pallas_call(
        kernel,
        out_shape=[jax.ShapeDtypeStruct(shape, kind) for shape, kind in zip(outs, kinds)],
        in_specs=[HBM] * in_hbm + [VMEM] * (len(operands) - in_hbm),
        out_specs=[VMEM] * len(outs),
        scratch_shapes=scratch_shapes,
        compiler_params=pltpu.CompilerParams(vmem_limit_bytes=16 * 1024 * 1024),
        cost_estimate=pl.CostEstimate(flops=10**9, bytes_accessed=NP * M1 * W * 4, transcendentals=0),
    )(*[pltpu.with_memory_space_constraint(x, pltpu.HBM) for x in operands[:in_hbm]], *operands[in_hbm:])


def exchange(x, axes, rows, head):
    peers = x.shape[0] // rows
    order = list(range(peers))
    order[0], order[head] = head, 0
    x = x.reshape(peers, rows, 1, W)
    x = lax.all_to_all(x, axes, 0, 0, axis_index_groups=[order])
    return x.reshape(peers * rows, W)


def per_device(tensor, factor_a, factor_b, factor_c):
    s1 = pl.pallas_call(
        pack_kernel,
        out_shape=pltpu.VMEM((NP * M1, W), F32),
        in_specs=[HBM] * 2,
        out_specs=VMEM,
        scratch_shapes=[
            pltpu.VMEM((2, R), F32),
            pltpu.VMEM((8, R), F32),
            pltpu.SemaphoreType.DMA((2,)),
        ],
        compiler_params=pltpu.CompilerParams(vmem_limit_bytes=16 * 1024 * 1024),
        cost_estimate=pl.CostEstimate(flops=10**9, bytes_accessed=NP * M1 * W * 4, transcendentals=0),
    )(*[pltpu.with_memory_space_constraint(x, pltpu.HBM) for x in (factor_b, factor_c)])
    block = tensor
    r1 = exchange(s1, ("ia", "ja"), M1, HEAD_P)
    s2, cc = call(
        second_kernel,
        [(NK * M2, W), (ROWS, W)],
        (block, factor_a, r1),
        [(ROWS, W), (16, W), (R, W)],
        kinds=[F32, BF16],
    )
    r2 = exchange(s2, "ka", M2, HEAD_K)
    (s3,) = call(
        third_kernel,
        [(NP * M3, W)],
        (block, factor_a, cc, r1, r2),
        [(ROWS, W), (ROWS, W)],
    )
    r3 = exchange(s3, ("ia", "ja"), M3, HEAD_P)
    return tuple(call(final_kernel, [(2, R), (8, R)], (r3,)))


def solution(mesh):
    placed = (P("ia", "ja", "ka"), P(), P(("ja", "ia", "ka"), None), P(("ka", "ia", "ja"), None))
    return jax.shard_map(
        per_device,
        mesh=mesh,
        in_specs=placed,
        out_specs=(P(("ja", "ia", "ka"), None), P(("ka", "ia", "ja"), None)),
        check_vma=False,
    )
```
